128 devices in a mesh: ctx: 16 (over z_hi, x, core), exp: 8 (over z_lo, y).
Axes of the slice: x: 4, y: 4, z: 4 (z_hi: 2, z_lo: 2; z = z_hi * 2 + z_lo), core: 2. Of those that a mesh axis runs over, the one named last changes fastest.
Arguments:
- queries: bfloat16 [2, 8192, 5120], P(None, 'ctx', 'exp'), may hold values from -5 to 5
- common_keys: bfloat16 [8192, 1024], P('ctx', 'exp'), may hold values from -5 to 5
- common_values: bfloat16 [8192, 1024], P('ctx', 'exp'), may hold values from -6 to 6
- doc_ids: int32 [8192], replicated, may hold values from 0 to 5, never falling along the last dimension, each value on 1 to 4096 neighbouring positions
- routes: int32 [8192, 1], P('ctx'), may hold values from 0 to 15, as said below
- residual: bfloat16 [8192, 6400], P('ctx', 'exp'), may hold values from -6 to 6
- out_weight: bfloat16 [5120, 6400], P('exp'), may hold values from -0.078125 to 0.078125
- norm_gain: float32 [6400], replicated, may hold values from 0.25 to 1.75
- gate_weight: bfloat16 [8, 6400, 4608], P('exp', None, 'ctx'), may hold values from -0.078125 to 0.078125
- up_weight: bfloat16 [8, 6400, 4608], P('exp', None, 'ctx'), may hold values from -0.078125 to 0.078125
- down_weight: bfloat16 [8, 4608, 6400], P('exp', 'ctx'), may hold values from -0.0625 to 0.0625
Outputs:
- first_attention: bfloat16 [8192, 5120], P('ctx', 'exp')
- expert_output: bfloat16 [8192, 6400], P('ctx', 'exp')
The draws below stay inside these ranges and needn't reach their ends.
Inputs may be any that keep to these rules, and one draw needn't show every extreme that they name: `routes`: in each aligned block of 512 rows every expert is named at most 40 times; one expert below 4 is named exactly 40 times in every block.
All inputs are finite; a program needn't handle non-finite values.
Results may differ from the reference program's by a relative error of at most 0.014.
Values may be sent and summed in bfloat16 or wider, within the bound.
No kernel may reach another device: no remote copies, remote signals or barrier semaphores. Data moves between devices by JAX's collectives and lax.ppermute only.
A program may use at most 128 MiB of HBM per device.

```python
import math
import jax
import jax.numpy as jnp
import numpy as np
from jax import lax

D = 6400
QUERY_HEAD_COUNT = 40
SHARED_KV_HEADS = 8
HEAD_WIDTH = 128
HID = 9216
N_ROUTED = 16
TOK_CTX = 512
DOCS = 6
SEQUENCE_LENGTH = 8192
CAP = 40
FLIGHT = 4


def draw_common_keys(key, part):
    key = jax.random.fold_in(key, 3)
    sampled_values = jnp.clip(jax.random.normal(key, (SEQUENCE_LENGTH, SHARED_KV_HEADS * HEAD_WIDTH), jnp.float32), -5.0, 5.0)
    return sampled_values.astype(jnp.bfloat16)


def draw_queries(key, part):
    key = jax.random.fold_in(key, 5)
    sampled_values = jnp.clip(2.0 * jax.random.normal(key, (2, SEQUENCE_LENGTH, QUERY_HEAD_COUNT * HEAD_WIDTH), jnp.float32), -5.0, 5.0)
    return sampled_values.astype(jnp.bfloat16)


def draw_routes(key, part):
    key = jax.random.fold_in(key, 11)
    favored = jax.random.randint(jax.random.fold_in(key, 1), (), 0, FLIGHT).astype(jnp.int32)
    others = jnp.arange(N_ROUTED - 1, dtype=jnp.int32)
    others = others + (others >= favored).astype(jnp.int32)
    supply = jnp.repeat(others, CAP)

    def one_block(number):
        block_key = jax.random.fold_in(key, number + 2)
        mixed = jax.random.permutation(jax.random.fold_in(block_key, 0), supply)[:TOK_CTX - CAP]
        filled = jnp.concatenate([jnp.full((CAP,), favored, jnp.int32), mixed])
        return jax.random.permutation(jax.random.fold_in(block_key, 1), filled)
    blocks = jax.vmap(one_block)(jnp.arange(SEQUENCE_LENGTH // TOK_CTX, dtype=jnp.int32))
    return blocks.reshape(SEQUENCE_LENGTH, 1).astype(jnp.int32)


def shard_levels(own_key, dims, shards, smallest, largest):
    def one(dim, shards_of):
        steps = jax.random.uniform(jax.random.fold_in(jax.random.fold_in(own_key, 6), dim), (shards_of,), jnp.float32, smallest / len(shards), largest / len(shards))
        return jnp.repeat(jnp.exp(steps), dims[dim] // shards_of).reshape((-1,) + (1,) * (len(dims) - dim - 1))

    level = one(*shards[0])
    for cut in shards[1:]:
        level = level * one(*cut)
    return level


def split_up(count, total, reach, skew):
    loads = [(1 << 20) // math.isqrt(grade ** skew) + 1 for grade in range(2, count + 1)]
    rest, counts = total - reach - (count - 1), [1] * (count - 1)
    while rest > 0:
        free = [i for i in range(count - 1) if counts[i] < reach]
        whole, left = sum([loads[i] for i in free]), rest
        for i in free:
            extra = min(reach - counts[i], max(1, left * loads[i] // whole), rest)
            counts[i] = counts[i] + extra
            rest = rest - extra
    return np.array([reach] + counts)


def uneven(rng, number_of, total, limit, skew):
    if number_of == 2:
        one = jax.random.randint(rng, (), max(1, total - limit), min(limit, total - 1) + 1)
        return jnp.stack([one, total - one])
    tallies = jnp.asarray(split_up(number_of, total, limit, skew), jnp.int32)
    pairs = (number_of - 1) // 2
    source_of, sink = tallies[1:1 + 2 * pairs:2], tallies[2:2 + 2 * pairs:2]
    room = jnp.minimum(source_of - 1, limit - sink)
    moved = jax.random.randint(jax.random.fold_in(rng, 1), (pairs,), 0, 1 << 20) % (room + 1)
    tallies = tallies.at[1:1 + 2 * pairs:2].set(source_of - moved).at[2:2 + 2 * pairs:2].set(sink + moved)
    return tallies[jax.random.permutation(jax.random.fold_in(rng, 2), number_of)]


def normal_values(own_key, dims, width, limit, shards=(), kind=jnp.bfloat16):
    drawn = jax.random.normal(own_key, dims, jnp.float32) * width
    if len(shards) > 0:
        drawn = shard_levels(own_key, dims, shards, -0.22, 0.18) * drawn
    return jnp.clip(drawn, min=-limit, max=limit).astype(kind)


def setup_inputs(seed: int = 0) -> dict:
    arg_keys = jax.random.split(jax.random.key(seed), 12)
    return {
        "queries": draw_queries(jax.random.fold_in(arg_keys[11], 71), 0),
        "common_keys": draw_common_keys(jax.random.fold_in(arg_keys[11], 71), 0),
        "common_values": normal_values(arg_keys[2], (SEQUENCE_LENGTH, SHARED_KV_HEADS * HEAD_WIDTH), 1.0, 6.0, ((0, 16), (1, 8))),
        "doc_ids": jnp.searchsorted(jnp.cumsum(uneven(arg_keys[3], DOCS, SEQUENCE_LENGTH, SEQUENCE_LENGTH // 2, 2)), jnp.arange(SEQUENCE_LENGTH), side="right").astype(jnp.int32),
        "routes": draw_routes(jax.random.fold_in(arg_keys[11], 71), 0),
        "residual": normal_values(arg_keys[5], (SEQUENCE_LENGTH, D), 0.5, 6.0, ((0, 16), (1, 8))),
        "out_weight": normal_values(arg_keys[6], (QUERY_HEAD_COUNT * HEAD_WIDTH, D), (QUERY_HEAD_COUNT * HEAD_WIDTH) ** -0.5, 0.078125, ((0, 8),)),
        "norm_gain": jnp.clip(1.0 + 0.15 * jax.random.normal(arg_keys[7], (D,), jnp.float32), 0.25, 1.75),
        "gate_weight": normal_values(arg_keys[8], (2 * FLIGHT, D, HID // 2), D ** -0.5, 0.078125, ((0, 8), (2, 16))),
        "up_weight": normal_values(arg_keys[9], (2 * FLIGHT, D, HID // 2), D ** -0.5, 0.078125, ((0, 8), (2, 16))),
        "down_weight": normal_values(arg_keys[10], (2 * FLIGHT, HID // 2, D), HID ** -0.5, 0.0625, ((0, 8), (1, 16))),
    }


big_negative = -1e+30
norm_eps = 1e-06

def layer_attention(query_layer, common_keys, common_values, visible):
    group_width = QUERY_HEAD_COUNT // SHARED_KV_HEADS
    query_heads = query_layer.reshape(SEQUENCE_LENGTH, QUERY_HEAD_COUNT, HEAD_WIDTH).transpose(1, 0, 2)
    key_head_rows = common_keys.reshape(SEQUENCE_LENGTH, SHARED_KV_HEADS, HEAD_WIDTH).transpose(1, 0, 2)
    value_head_rows = common_values.reshape(SEQUENCE_LENGTH, SHARED_KV_HEADS, HEAD_WIDTH).transpose(1, 0, 2)
    score_scale = float(HEAD_WIDTH) ** (-0.5)

    def one_head(head):
        query_head = lax.dynamic_index_in_dim(query_heads, head, 0, keepdims=False)
        key_head = lax.dynamic_index_in_dim(key_head_rows, head // group_width, 0, keepdims=False)
        value_head = lax.dynamic_index_in_dim(value_head_rows, head // group_width, 0, keepdims=False)
        scores = jnp.dot(query_head, key_head.T, preferred_element_type=jnp.float32) * score_scale
        scores = jnp.where(visible, scores, big_negative)
        highest = lax.optimization_barrier(jnp.max(scores, axis=1, keepdims=True))
        probs = jnp.where(visible, jnp.exp(scores - highest), 0.0)
        totals = lax.optimization_barrier(jnp.sum(probs, axis=1, keepdims=True))
        summed = jnp.dot(probs.astype(jnp.bfloat16), value_head, preferred_element_type=jnp.float32)
        return (summed / totals).astype(jnp.bfloat16)
    heads_out = lax.map(one_head, jnp.arange(QUERY_HEAD_COUNT, dtype=jnp.int32))
    return heads_out.transpose(1, 0, 2).reshape(SEQUENCE_LENGTH, QUERY_HEAD_COUNT * HEAD_WIDTH)

def reference(queries, common_keys, common_values, doc_ids, routes, residual, out_weight, norm_gain, gate_weight, up_weight, down_weight):
    positions = jnp.arange(SEQUENCE_LENGTH, dtype=jnp.int32)
    visible = (positions[None, :] <= positions[:, None]) & (doc_ids[None, :] == doc_ids[:, None])
    first_attention = layer_attention(queries[0], common_keys, common_values, visible)
    second_mix = layer_attention(queries[1], common_keys, common_values, visible)
    block_count = SEQUENCE_LENGTH // TOK_CTX
    route_ids = routes[:, 0]
    shard_ids = positions // TOK_CTX
    chosen = (route_ids[:, None] == jnp.arange(FLIGHT, dtype=jnp.int32)[None, :]).astype(jnp.int32)
    ranking = jnp.cumsum(chosen.reshape(block_count, TOK_CTX, FLIGHT), axis=1).reshape(SEQUENCE_LENGTH, FLIGHT) - 1
    token_rank = lax.optimization_barrier(jnp.sum(ranking * chosen, axis=1))
    in_flight = route_ids < FLIGHT
    slot_total = FLIGHT * block_count * CAP
    slot_place = jnp.where(in_flight, (route_ids * block_count + shard_ids) * CAP + token_rank, slot_total).astype(jnp.int32)
    slot_token = jnp.zeros((slot_total,), jnp.int32).at[slot_place].set(positions, mode='drop')
    state = residual.astype(jnp.float32) + jnp.dot(second_mix, out_weight, preferred_element_type=jnp.float32)
    mean_square = lax.optimization_barrier(jnp.mean(state * state, axis=1, keepdims=True))
    normed = (state * lax.rsqrt(mean_square + norm_eps) * norm_gain).astype(jnp.bfloat16)
    gathered = jnp.take(normed, slot_token, axis=0).reshape(FLIGHT, block_count * CAP, D)
    outputs = []
    for expert in range(FLIGHT):
        gate_full = jnp.concatenate([gate_weight[2 * expert], gate_weight[2 * expert + 1]], axis=1)
        up_full = jnp.concatenate([up_weight[2 * expert], up_weight[2 * expert + 1]], axis=1)
        down_full = jnp.concatenate([down_weight[2 * expert], down_weight[2 * expert + 1]], axis=0)
        rows_in = gathered[expert]
        gate_value = jnp.dot(rows_in, gate_full, preferred_element_type=jnp.float32)
        up_value = jnp.dot(rows_in, up_full, preferred_element_type=jnp.float32)
        activations = (jax.nn.silu(gate_value) * up_value).astype(jnp.bfloat16)
        outputs.append(jnp.dot(activations, down_full, preferred_element_type=jnp.float32).astype(jnp.bfloat16))
    slot_values = jnp.concatenate(outputs, axis=0)
    picked = jnp.take(slot_values, jnp.minimum(slot_place, slot_total - 1), axis=0)
    expert_output = jnp.where(in_flight[:, None], picked, jnp.zeros_like(picked))
    return (first_attention, expert_output)
```

```python
import functools

import jax
import jax.numpy as jnp
from jax import lax
from jax.experimental import pallas as pl
from jax.experimental.pallas import tpu as pltpu
from jax.sharding import PartitionSpec as P

QUERY_HEAD_COUNT = 40
SHARED_KV_HEADS = 8
HEAD_WIDTH = 128
CAP = 40

GROUP = QUERY_HEAD_COUNT // SHARED_KV_HEADS
BLOCK = 512
BACK = 4
KV_SLOTS = 2 * (BACK + 1)
PADDED_CAP = 48
HALF = PADDED_CAP // 2
SPLIT = 16
MIB = 1 << 20

big_negative = -1e30
norm_eps = 1e-06
log2e = 1.4426950408889634

VMEM = pl.BlockSpec(memory_space=pltpu.VMEM)
SMEM = pl.BlockSpec(memory_space=pltpu.SMEM)
ANY = pl.BlockSpec(memory_space=pl.ANY)


def flash(scalars, query, low, high, blocks, keys, values, bias, highest, numer):
    first, last, core, base = scalars[0], scalars[1], scalars[2], scalars[3]
    rows = query.shape[0]
    for back in range(BACK + 1):
        for block, place in ((blocks[back], core), (blocks[BACK + 1 + back], 1 - core)):
            at = 2 * (BACK - back) + place
            keys[at] = block[:, :HEAD_WIDTH]
            values[at, :, :HEAD_WIDTH] = block[:, HEAD_WIDTH:]
            values[at, :, HEAD_WIDTH:] = jnp.ones((BLOCK, HEAD_WIDTH), jnp.bfloat16)
    highest[...] = jnp.full(highest.shape, big_negative, jnp.float32)
    numer[...] = jnp.zeros(numer.shape, jnp.float32)
    scale = float(HEAD_WIDTH) ** (-0.5) * log2e

    def step(at, carry):
        place = (base + at) * BLOCK + lax.broadcasted_iota(jnp.int32, (rows, BLOCK), 1)
        seen = (place >= low) & (place <= high)
        bias[...] = jnp.where(seen, 0.0, big_negative)
        key_block = keys[at]
        value_block = values[at]
        for head in range(GROUP):
            scores = lax.dot_general(
                query[:, head * HEAD_WIDTH : (head + 1) * HEAD_WIDTH],
                key_block,
                (((1,), (1,)), ((), ())),
                preferred_element_type=jnp.float32,
            )
            scores = scores + bias[...]
            old = highest[head]
            new = jnp.maximum(old, jnp.max(scores, axis=1, keepdims=True))
            probs = jnp.exp2((scores - new) * scale).astype(jnp.bfloat16)
            factor = jnp.exp2((old - new) * scale)
            highest[head] = new
            numer[head] = numer[head] * factor + jnp.dot(
                probs, value_block, preferred_element_type=jnp.float32
            )
        return carry

    lax.fori_loop(first, last + 1, step, 0)


def store_heads(numer, out):
    for head in range(GROUP):
        summed = numer[head]
        out[:, head * HEAD_WIDTH : (head + 1) * HEAD_WIDTH] = (
            summed[:, :HEAD_WIDTH] / summed[:, HEAD_WIDTH:]
        ).astype(jnp.bfloat16)


def flash_scratch(rows):
    return [
        pltpu.VMEM((KV_SLOTS, BLOCK, HEAD_WIDTH), jnp.bfloat16),
        pltpu.VMEM((KV_SLOTS, BLOCK, 2 * HEAD_WIDTH), jnp.bfloat16),
        pltpu.VMEM((rows, BLOCK), jnp.float32),
        pltpu.VMEM((GROUP, rows, 1), jnp.float32),
        pltpu.VMEM((GROUP, rows, 2 * HEAD_WIDTH), jnp.float32),
    ]


def flash_cost(rows, more_flops, more_bytes):
    typical = 6
    return pl.CostEstimate(
        flops=typical * GROUP * rows * BLOCK * HEAD_WIDTH * 8 + more_flops,
        bytes_accessed=KV_SLOTS * BLOCK * HEAD_WIDTH * 4 + more_bytes,
        transcendentals=typical * GROUP * rows * BLOCK,
    )


def first_kernel(scalars, query, low, *refs):
    blocks = refs[:KV_SLOTS]
    out, keys, values, bias, highest, numer = refs[-6:]
    rows = query.shape[0]
    start = (scalars[3] + scalars[1]) * BLOCK
    high = start + lax.broadcasted_iota(jnp.int32, (rows, 1), 0)
    flash(scalars, query, low[...], high, blocks, keys, values, bias, highest, numer)
    store_heads(numer, out)


def attend_first(scalars, queries, low, blocks, after):
    _, rows, width = queries.shape
    return pl.pallas_call(
        first_kernel,
        grid=(1,),
        out_shape=jax.ShapeDtypeStruct((rows, width), jnp.bfloat16),
        in_specs=[SMEM, pl.BlockSpec((None, rows, width), lambda i: (0, 0, 0)), VMEM]
        + [VMEM] * KV_SLOTS
        + [ANY] * len(after),
        out_specs=pl.BlockSpec((rows, width), lambda i: (0, 0)),
        scratch_shapes=flash_scratch(rows),
        compiler_params=pltpu.CompilerParams(vmem_limit_bytes=40 * MIB),
        cost_estimate=flash_cost(rows, 0, 4 * rows * width),
    )(scalars, queries, low, *blocks, *after)


def slots_kernel(scalars, query, table, low, residual, weight, *refs):
    blocks = refs[:KV_SLOTS]
    out, keys, values, bias, highest, numer, picked, mix, product = refs[KV_SLOTS:]
    rows, tokens = table.shape
    features = residual.shape[0]
    chosen = table[...]
    picked[...] = jnp.dot(chosen, query[...], preferred_element_type=jnp.float32).astype(
        jnp.bfloat16
    )
    start = (scalars[3] + scalars[1]) * BLOCK
    place = start + lax.broadcasted_iota(jnp.int32, (1, tokens), 1)
    held = chosen.astype(jnp.float32)
    slot_low = jnp.sum(held * low[...].astype(jnp.float32), axis=1, keepdims=True)
    slot_high = jnp.sum(held * place.astype(jnp.float32), axis=1, keepdims=True)
    slot_low = slot_low.astype(jnp.int32)
    slot_high = jnp.maximum(slot_high.astype(jnp.int32), start)
    flash(scalars, picked, slot_low, slot_high, blocks, keys, values, bias, highest, numer)
    store_heads(numer, mix)
    product[...] = jnp.dot(mix[...], weight[...], preferred_element_type=jnp.float32)
    slot_resid = lax.dot_general(
        chosen, residual[...], (((1,), (1,)), ((), ())), preferred_element_type=jnp.float32
    )
    for part in range(product.shape[1] // features):

        @pl.when(scalars[4] == part)
        def _():
            product[:, part * features : (part + 1) * features] += slot_resid

    out[...] = product[...].astype(jnp.bfloat16)


def attend_slots(scalars, queries, table, low, residual, weight, blocks):
    _, tokens, width = queries.shape
    rows = table.shape[0]
    out_width = weight.shape[1]
    return pl.pallas_call(
        slots_kernel,
        grid=(1,),
        out_shape=jax.ShapeDtypeStruct((rows, out_width), jnp.bfloat16),
        in_specs=[SMEM, pl.BlockSpec((None, tokens, width), lambda i: (1, 0, 0))]
        + [VMEM] * (4 + KV_SLOTS),
        out_specs=pl.BlockSpec((rows, out_width), lambda i: (0, 0)),
        scratch_shapes=flash_scratch(rows)
        + [
            pltpu.VMEM((rows, width), jnp.bfloat16),
            pltpu.VMEM((rows, width), jnp.bfloat16),
            pltpu.VMEM((rows, out_width), jnp.float32),
        ],
        compiler_params=pltpu.CompilerParams(vmem_limit_bytes=48 * MIB),
        cost_estimate=flash_cost(rows, 2 * rows * width * out_width, 2 * width * out_width),
    )(scalars, queries, table, low, residual, weight, *blocks)


def norm_kernel(shares, gain, *refs):
    out = refs[-1]
    state = shares[0].astype(jnp.float32)
    for number in range(1, shares.shape[0]):
        state = state + shares[number].astype(jnp.float32)
    mean_square = jnp.mean(state * state, axis=1, keepdims=True)
    out[...] = (state * lax.rsqrt(mean_square + norm_eps) * gain[...]).astype(jnp.bfloat16)


def normalize(shares, norm_gain, after):
    count, rows, width = shares.shape
    return pl.pallas_call(
        norm_kernel,
        out_shape=jax.ShapeDtypeStruct((rows, width), jnp.bfloat16),
        in_specs=[VMEM, VMEM] + [ANY] * len(after),
        out_specs=VMEM,
        compiler_params=pltpu.CompilerParams(vmem_limit_bytes=24 * MIB),
        cost_estimate=pl.CostEstimate(
            flops=count * rows * width * 3,
            bytes_accessed=(count + 1) * rows * width * 2,
            transcendentals=rows,
        ),
    )(shares, norm_gain.reshape(1, width), *after)


def hidden_kernel(offsets, *refs):
    pieces = len(offsets)
    rows_in, weights_in = refs[:pieces], refs[pieces : pieces + 4]
    act, rows, weights, total = refs[pieces + 4 :]
    step = pl.program_id(0)
    units = weights_in[0].shape[0]

    @pl.when(step == 0)
    def _():
        rows[...] = jnp.zeros(rows.shape, jnp.bfloat16)
        total[...] = jnp.zeros(total.shape, jnp.float32)

    for offset, piece in zip(offsets, rows_in):
        rows[offset : offset + piece.shape[0], :] = piece[...]
    for number in range(4):
        weights[number * units : (number + 1) * units, :] = weights_in[number][...]
    total[...] += lax.dot_general(
        rows[...],
        weights[...],
        (((1,), (1,)), ((), ())),
        preferred_element_type=jnp.float32,
    )

    @pl.when(step == pl.num_programs(0) - 1)
    def _():
        gate = total[:, : 2 * units]
        up = total[:, 2 * units :]
        act[...] = (gate / (1.0 + jnp.exp(-gate)) * up).astype(jnp.bfloat16)


def hidden(row_pieces, weights):
    offsets, flat = [], []
    for number, parts in enumerate(row_pieces):
        offset = number * PADDED_CAP
        for part in parts:
            offsets.append(offset)
            flat.append(part)
            offset += part.shape[0]
    width = flat[0].shape[1]
    units = weights[0].shape[0]
    rows = len(row_pieces) * PADDED_CAP
    chunk = 1280
    weight_spec = pl.BlockSpec((units, chunk), lambda i: (0, i))
    return pl.pallas_call(
        functools.partial(hidden_kernel, tuple(offsets)),
        grid=(width // chunk,),
        out_shape=jax.ShapeDtypeStruct((rows, 2 * units), jnp.bfloat16),
        in_specs=[pl.BlockSpec((part.shape[0], chunk), lambda i: (0, i)) for part in flat]
        + [weight_spec] * 4,
        out_specs=pl.BlockSpec((rows, 2 * units), lambda i: (0, 0)),
        scratch_shapes=[
            pltpu.VMEM((rows, chunk), jnp.bfloat16),
            pltpu.VMEM((4 * units, chunk), jnp.bfloat16),
            pltpu.VMEM((rows, 4 * units), jnp.float32),
        ],
        compiler_params=pltpu.CompilerParams(vmem_limit_bytes=40 * MIB),
        cost_estimate=pl.CostEstimate(
            flops=8 * rows * width * units,
            bytes_accessed=2 * rows * width + 8 * width * units,
            transcendentals=2 * rows * units,
        ),
    )(*flat, *weights)


def down_kernel(places, act, down_own, down_other, out, weights, product):
    units = down_own.shape[0]
    pieces = out.shape[0]
    features = out.shape[3]
    weights[:units, :] = down_own[...]
    weights[units:, :] = down_other[...]
    product[...] = jnp.dot(act[...], weights[...], preferred_element_type=jnp.float32)
    for number in range(pieces):
        place = places[number]
        for part in range(out.shape[1]):
            out[place, part] = product[
                number * PADDED_CAP : number * PADDED_CAP + CAP,
                part * features : (part + 1) * features,
            ].astype(jnp.bfloat16)


def down(places, act, downs, parts):
    rows = act.shape[0]
    units, width = downs[0].shape
    pieces = rows // PADDED_CAP
    features = width // parts
    steps = 2
    weight_spec = pl.BlockSpec((units, width // steps), lambda i: (0, i))
    return pl.pallas_call(
        down_kernel,
        grid=(steps,),
        out_shape=jax.ShapeDtypeStruct((pieces, parts, CAP, features), jnp.bfloat16),
        in_specs=[SMEM, pl.BlockSpec(act.shape, lambda i: (0, 0)), weight_spec, weight_spec],
        out_specs=pl.BlockSpec((pieces, parts // steps, CAP, features), lambda i: (0, i, 0, 0)),
        scratch_shapes=[
            pltpu.VMEM((2 * units, width // steps), jnp.bfloat16),
            pltpu.VMEM((rows, width // steps), jnp.float32),
        ],
        compiler_params=pltpu.CompilerParams(vmem_limit_bytes=48 * MIB),
        cost_estimate=pl.CostEstimate(
            flops=4 * rows * width * units,
            bytes_accessed=2 * rows * width + 4 * width * units,
            transcendentals=0,
        ),
    )(places, act, *downs)


def collect_kernel(shares, table, out, merged):
    step = pl.program_id(0)
    sources, _, halves, rows, features = shares.shape
    total = jnp.zeros((rows, features), jnp.float32)
    for source in range(sources):
        for half in range(halves):
            total = total + shares[source, 0, half].astype(jnp.float32)
    spare = jnp.zeros((PADDED_CAP - rows, features), jnp.float32)
    merged[step] = jnp.concatenate([total, spare], axis=0).astype(jnp.bfloat16)

    @pl.when(step == pl.num_programs(0) - 1)
    def _():
        experts = merged.shape[0]
        stacked = merged[...].reshape(experts * PADDED_CAP, features)
        out[...] = lax.dot_general(
            stacked, table[...], (((0,), (0,)), ((), ())), preferred_element_type=jnp.float32
        ).astype(jnp.bfloat16)


def collect(shares, table):
    sources, experts, halves, rows, features = shares.shape
    tokens = table.shape[1]
    return pl.pallas_call(
        collect_kernel,
        grid=(experts,),
        out_shape=jax.ShapeDtypeStruct((features, tokens), jnp.bfloat16),
        in_specs=[
            pl.BlockSpec((sources, 1, halves, rows, features), lambda i: (0, i, 0, 0, 0)),
            pl.BlockSpec(table.shape, lambda i: (0, 0)),
        ],
        out_specs=pl.BlockSpec((features, tokens), lambda i: (0, 0)),
        scratch_shapes=[pltpu.VMEM((experts, PADDED_CAP, features), jnp.bfloat16)],
        compiler_params=pltpu.CompilerParams(vmem_limit_bytes=24 * MIB),
        cost_estimate=pl.CostEstimate(
            flops=2 * tokens * table.shape[0] * features,
            bytes_accessed=2 * shares.size + 2 * tokens * features,
            transcendentals=0,
        ),
    )(shares, table)


def shards(
    queries,
    common_keys,
    common_values,
    doc_ids,
    routes,
    residual,
    out_weight,
    norm_gain,
    gate_weight,
    up_weight,
    down_weight,
):
    ctx_size = lax.axis_size("ctx")
    exp_size = lax.axis_size("exp")
    chips = ctx_size // 2
    in_flight = exp_size // 2
    tokens = queries.shape[1]
    features = residual.shape[1]
    ctx = lax.axis_index("ctx")
    exp = lax.axis_index("exp")
    chip, core = ctx // 2, ctx % 2
    swap_cores = [(c, c ^ 1) for c in range(ctx_size)]

    own = jnp.concatenate([common_keys, common_values], axis=1)
    mine = [own] + [
        lax.ppermute(own, "ctx", [(c, c + 2 * s) for c in range(ctx_size - 2 * s)])
        for s in range(1, BACK + 1)
    ]
    theirs = [lax.ppermute(block, "ctx", swap_cores) for block in mine]

    blocks = mine + theirs
    query_docs = lax.dynamic_slice_in_dim(doc_ids, ctx * tokens, tokens)
    doc_numbers = jnp.arange(6, dtype=jnp.int32)
    starts = jnp.sum((doc_ids[None, :] < doc_numbers[:, None]).astype(jnp.int32), axis=1)
    low = jnp.sum(
        jnp.where(query_docs[None, :] == doc_numbers[:, None], starts[:, None], 0), axis=0
    )
    base = 2 * (chip - BACK)
    scalars = jnp.stack([low[0] // BLOCK - base, 2 * BACK + core, core, base, exp])
    scalars = scalars.astype(jnp.int32)

    route_ids = routes.reshape(1, tokens)
    chosen = (route_ids == jnp.arange(in_flight, dtype=jnp.int32)[:, None]).astype(jnp.int32)
    ranking = jnp.cumsum(chosen, axis=1) - 1
    placed = (chosen[:, None, :] == 1) & (
        ranking[:, None, :] == jnp.arange(PADDED_CAP, dtype=jnp.int32)[None, :, None]
    )
    table = placed.reshape(in_flight * PADDED_CAP, tokens).astype(jnp.bfloat16)

    product = attend_slots(
        scalars, queries, table, low.reshape(1, tokens), residual.T, out_weight, blocks
    )
    shares = lax.all_to_all(
        product.reshape(exp_size, HALF, exp_size * features), "exp", 0, 0, tiled=True
    )
    first_attention = attend_first(
        scalars, queries, low.reshape(tokens, 1), blocks, after=(product,)
    )
    gate, up, down_own = gate_weight[0].T, up_weight[0].T, down_weight[0]
    gate, up, down_own, _ = lax.optimization_barrier((gate, up, down_own, product))
    gate_other, up_other, down_other = (
        lax.ppermute(weight, "ctx", swap_cores) for weight in (gate, up, down_own)
    )
    normed = normalize(shares, norm_gain, after=(gate_other, up_other, down_other, first_attention))

    pair = [(e, e ^ 1) for e in range(exp_size)]
    other = lax.ppermute(normed, "exp", pair)
    odd = exp % 2 == 1
    block = jnp.concatenate(
        [jnp.where(odd, other, normed), jnp.where(odd, normed, other)[: CAP - HALF]], axis=0
    )
    ring = chips // 2

    def beside(c, distance):
        chip_of, core_of = c // 2, c % 2
        place = (chip_of % ring + distance) % ring
        return (chip_of // ring * ring + place) * 2 + core_of

    right = [(c, beside(c, 1)) for c in range(ctx_size)]
    left = [(c, beside(c, -1)) for c in range(ctx_size)]
    across = [(c, (c + ctx_size // 2) % ctx_size) for c in range(ctx_size)]
    from_left = lax.ppermute(block, "ctx", right)
    from_right = lax.ppermute(block, "ctx", left)
    far = lax.ppermute(block, "ctx", across)
    opposite_top = lax.ppermute(from_left[:SPLIT], "ctx", right)
    opposite_rest = lax.ppermute(from_right[SPLIT:], "ctx", left)
    far_left = lax.ppermute(far, "ctx", right)
    far_right = lax.ppermute(far, "ctx", left)
    far_opposite_top = lax.ppermute(opposite_top, "ctx", across)
    far_opposite_rest = lax.ppermute(opposite_rest, "ctx", across)
    pieces = [
        (block,),
        (far,),
        (from_left,),
        (from_right,),
        (far_left,),
        (far_right,),
        (opposite_top, opposite_rest),
        (far_opposite_top, far_opposite_rest),
    ]
    row, along = chip // ring, chip % ring
    places = jnp.stack(
        [
            (row ^ z) * ring + (along + x) % ring
            for z, x in (
                (0, 0), (1, 0), (0, ring - 1), (0, 1), (1, ring - 1), (1, 1), (0, 2), (1, 2)
            )
        ]
    ).astype(jnp.int32)

    act = hidden(pieces, (gate, gate_other, up, up_other))
    partial = down(places, act, (down_own, down_other), exp_size)
    same_core = [
        [c * exp_size + e for c in range(k, ctx_size, 2) for e in range(exp_size)]
        for k in range(2)
    ]
    returned = lax.all_to_all(
        partial.reshape(chips * exp_size, CAP, features),
        ("ctx", "exp"),
        0,
        0,
        tiled=True,
        axis_index_groups=same_core,
    )
    expert_output = collect(returned.reshape(chips, in_flight, 2, CAP, features), table)
    return (first_attention, expert_output.T)


def solution(mesh):
    in_specs = (
        P(None, "ctx", "exp"),
        P("ctx", "exp"),
        P("ctx", "exp"),
        P(),
        P("ctx", None),
        P("ctx", "exp"),
        P("exp", None),
        P(),
        P("exp", None, "ctx"),
        P("exp", None, "ctx"),
        P("exp", "ctx", None),
    )
    out_specs = (P("ctx", "exp"), P("ctx", "exp"))
    return jax.shard_map(shards, mesh=mesh, in_specs=in_specs, out_specs=out_specs, check_vma=False)
```

```python
import functools

import jax
import jax.numpy as jnp
from jax import lax
from jax.experimental import pallas as pl
from jax.experimental.pallas import tpu as pltpu
from jax.sharding import PartitionSpec as P

QUERY_HEAD_COUNT = 40
SHARED_KV_HEADS = 8
HEAD_WIDTH = 128
CAP = 40

GROUP = QUERY_HEAD_COUNT // SHARED_KV_HEADS
BLOCK = 512
BACK = 4
KV_SLOTS = 2 * (BACK + 1)
PADDED_CAP = 48
HALF = PADDED_CAP // 2
SPLIT = 16
MIB = 1 << 20
SLOTS_VMEM = 50
TILE = 256

big_negative = -1e30
norm_eps = 1e-06
log2e = 1.4426950408889634

VMEM = pl.BlockSpec(memory_space=pltpu.VMEM)
SMEM = pl.BlockSpec(memory_space=pltpu.SMEM)
ANY = pl.BlockSpec(memory_space=pl.ANY)
TOKEN = jax.ShapeDtypeStruct((8, 128), jnp.float32)


def fetch(sources, targets, done):
    copies = [
        pltpu.make_async_copy(source, target, done.at[number])
        for number, (source, target) in enumerate(zip(sources, targets))
    ]
    for copy in copies:
        copy.start()
    return copies


def flash(scalars, query, low, high, pairs, bias, highest, numer):
    first, last, core, base = scalars[0], scalars[1], scalars[2], scalars[3]
    rows = query.shape[0]
    highest[...] = jnp.full(highest.shape, big_negative, jnp.float32)
    numer[...] = jnp.zeros(numer.shape, jnp.float32)
    scale = float(HEAD_WIDTH) ** (-0.5) * log2e
    ones = jnp.ones((BLOCK, HEAD_WIDTH), jnp.bfloat16)

    def step(at, carry):
        place = (base + at) * BLOCK + lax.broadcasted_iota(jnp.int32, (rows, BLOCK), 1)
        seen = (place >= low) & (place <= high)
        bias[...] = jnp.where(seen, 0.0, big_negative)
        slot = BACK - at // 2 + jnp.where(at % 2 == core, 0, BACK + 1)
        key_block = pairs[slot, :, :HEAD_WIDTH]
        value_block = jnp.concatenate([pairs[slot, :, HEAD_WIDTH:], ones], axis=1)
        tile = TILE if rows % TILE == 0 else rows
        for head in range(GROUP):
            for top in range(0, rows, tile):
                part = slice(top, top + tile)
                scores = lax.dot_general(
                    query[part, head * HEAD_WIDTH : (head + 1) * HEAD_WIDTH],
                    key_block,
                    (((1,), (1,)), ((), ())),
                    preferred_element_type=jnp.float32,
                )
                scores = scores + bias[part, :]
                old = highest[head, part]
                new = jnp.maximum(old, jnp.max(scores, axis=1, keepdims=True))
                probs = jnp.exp2((scores - new) * scale).astype(jnp.bfloat16)
                factor = jnp.exp2((old - new) * scale)
                highest[head, part] = new
                numer[head, part] = numer[head, part] * factor + jnp.dot(
                    probs, value_block, preferred_element_type=jnp.float32
                )
        return carry

    lax.fori_loop(first, last + 1, step, 0)


def store_heads(numer, out):
    for head in range(GROUP):
        summed = numer[head]
        out[:, head * HEAD_WIDTH : (head + 1) * HEAD_WIDTH] = (
            summed[:, :HEAD_WIDTH] / summed[:, HEAD_WIDTH:]
        ).astype(jnp.bfloat16)


def flash_scratch(rows, tokens, width):
    return [
        pltpu.VMEM((KV_SLOTS, BLOCK, 2 * HEAD_WIDTH), jnp.bfloat16),
        pltpu.VMEM((tokens, width), jnp.bfloat16),
        pltpu.VMEM((rows, BLOCK), jnp.float32),
        pltpu.VMEM((GROUP, rows, 1), jnp.float32),
        pltpu.VMEM((GROUP, rows, 2 * HEAD_WIDTH), jnp.float32),
        pltpu.SemaphoreType.DMA((KV_SLOTS + 2,)),
    ]


def flash_cost(rows, more_flops, more_bytes):
    typical = 6
    return pl.CostEstimate(
        flops=typical * GROUP * rows * BLOCK * HEAD_WIDTH * 8 + more_flops,
        bytes_accessed=KV_SLOTS * BLOCK * HEAD_WIDTH * 4 + more_bytes,
        transcendentals=typical * GROUP * rows * BLOCK,
    )


def first_kernel(scalars, queries, low, *refs):
    blocks = refs[:KV_SLOTS]
    out, token, pairs, query, bias, highest, numer, done = refs[-8:]
    token[...] = jnp.zeros(token.shape, jnp.float32)
    copies = fetch(
        [queries.at[0], *blocks], [query] + [pairs.at[n] for n in range(KV_SLOTS)], done
    )
    rows = query.shape[0]
    start = (scalars[3] + scalars[1]) * BLOCK
    high = start + lax.broadcasted_iota(jnp.int32, (rows, 1), 0)
    for copy in copies:
        copy.wait()
    flash(scalars, query, low[...], high, pairs, bias, highest, numer)
    store_heads(numer, out)


def attend_first(scalars, queries, low, blocks, after):
    _, rows, width = queries.shape
    return pl.pallas_call(
        first_kernel,
        out_shape=[jax.ShapeDtypeStruct((rows, width), jnp.bfloat16), TOKEN],
        in_specs=[SMEM, ANY, VMEM] + [ANY] * KV_SLOTS + [VMEM] * len(after),
        out_specs=[VMEM, VMEM],
        scratch_shapes=flash_scratch(rows, rows, width),
        compiler_params=pltpu.CompilerParams(vmem_limit_bytes=58 * MIB),
        cost_estimate=flash_cost(rows, 0, 4 * rows * width),
    )(scalars, queries, low, *blocks, *after)


def slots_kernel(scalars, queries, routes, low, residual, weight, *refs):
    blocks = refs[:KV_SLOTS]
    out, table, token, pairs, query, bias, highest, numer, done = refs[KV_SLOTS : KV_SLOTS + 9]
    picked, mix, product, features_in = refs[KV_SLOTS + 9 :]
    token[...] = jnp.zeros(token.shape, jnp.float32)
    copies = fetch(
        [queries.at[1], *blocks, residual],
        [query] + [pairs.at[n] for n in range(KV_SLOTS)] + [features_in],
        done,
    )
    rows, tokens = table.shape
    features = features_in.shape[0]
    route = routes[...]
    earlier = lax.broadcasted_iota(jnp.int32, (tokens, tokens), 0)
    earlier = earlier <= lax.broadcasted_iota(jnp.int32, (tokens, tokens), 1)
    named = lax.broadcasted_iota(jnp.int32, (16, tokens), 0) == route
    rank = jnp.dot(
        jnp.where(named, 1.0, 0.0).astype(jnp.bfloat16),
        jnp.where(earlier, 1.0, 0.0).astype(jnp.bfloat16),
        preferred_element_type=jnp.float32,
    )
    rank = rank.astype(jnp.int32) - 1
    number = lax.broadcasted_iota(jnp.int32, (PADDED_CAP, tokens), 0)
    for expert in range(rows // PADDED_CAP):
        placed = (rank[expert : expert + 1, :] == number) & (route == expert)
        table[expert * PADDED_CAP : (expert + 1) * PADDED_CAP, :] = jnp.where(
            placed, 1.0, 0.0
        ).astype(jnp.bfloat16)
    chosen = table[...]
    start = (scalars[3] + scalars[1]) * BLOCK
    place = start + lax.broadcasted_iota(jnp.int32, (1, tokens), 1)
    held = chosen.astype(jnp.float32)
    slot_low = jnp.sum(held * low[...].astype(jnp.float32), axis=1, keepdims=True)
    slot_high = jnp.sum(held * place.astype(jnp.float32), axis=1, keepdims=True)
    slot_low = slot_low.astype(jnp.int32)
    slot_high = jnp.maximum(slot_high.astype(jnp.int32), start)
    copies[0].wait()
    picked[...] = jnp.dot(chosen, query[...], preferred_element_type=jnp.float32).astype(
        jnp.bfloat16
    )
    for copy in copies[1 : KV_SLOTS + 1]:
        copy.wait()
    flash(scalars, picked, slot_low, slot_high, pairs, bias, highest, numer)
    store_heads(numer, mix)
    for copy in copies[KV_SLOTS + 1 :]:
        copy.wait()
    product[...] = jnp.dot(mix[...], weight[...], preferred_element_type=jnp.float32)
    slot_resid = lax.dot_general(
        chosen, features_in[...], (((1,), (1,)), ((), ())), preferred_element_type=jnp.float32
    )
    for part in range(product.shape[1] // features):

        @pl.when(scalars[4] == part)
        def _():
            product[:, part * features : (part + 1) * features] += slot_resid

    out[...] = product[...].astype(jnp.bfloat16)


def attend_slots(scalars, queries, routes, low, residual, weight, blocks, rows):
    _, tokens, width = queries.shape
    out_width = weight.shape[1]
    return pl.pallas_call(
        slots_kernel,
        out_shape=[
            jax.ShapeDtypeStruct((rows, out_width), jnp.bfloat16),
            jax.ShapeDtypeStruct((rows, tokens), jnp.bfloat16),
            TOKEN,
        ],
        in_specs=[SMEM, ANY, VMEM, VMEM, ANY, VMEM] + [ANY] * KV_SLOTS,
        out_specs=[VMEM, VMEM, VMEM],
        scratch_shapes=flash_scratch(rows, tokens, width)
        + [
            pltpu.VMEM((rows, width), jnp.bfloat16),
            pltpu.VMEM((rows, width), jnp.bfloat16),
            pltpu.VMEM((rows, out_width), jnp.float32),
            pltpu.VMEM(residual.shape, jnp.bfloat16),
        ],
        compiler_params=pltpu.CompilerParams(vmem_limit_bytes=SLOTS_VMEM * MIB),
        cost_estimate=flash_cost(rows, 2 * rows * width * out_width, 2 * width * out_width),
    )(scalars, queries, routes, low, residual, weight, *blocks)


def norm_kernel(shares, gain, *refs):
    out = refs[-1]
    state = shares[0].astype(jnp.float32)
    for number in range(1, shares.shape[0]):
        state = state + shares[number].astype(jnp.float32)
    mean_square = jnp.mean(state * state, axis=1, keepdims=True)
    out[...] = (state * lax.rsqrt(mean_square + norm_eps) * gain[...]).astype(jnp.bfloat16)


def normalize(shares, norm_gain, after):
    count, rows, width = shares.shape
    return pl.pallas_call(
        norm_kernel,
        out_shape=jax.ShapeDtypeStruct((rows, width), jnp.bfloat16),
        in_specs=[VMEM, VMEM] + [VMEM] * len(after),
        out_specs=VMEM,
        compiler_params=pltpu.CompilerParams(vmem_limit_bytes=24 * MIB),
        cost_estimate=pl.CostEstimate(
            flops=count * rows * width * 3,
            bytes_accessed=(count + 1) * rows * width * 2,
            transcendentals=rows,
        ),
    )(shares, norm_gain.reshape(1, width), *after)


def hidden_kernel(offsets, *refs):
    pieces = len(offsets)
    rows_in, weights_in = refs[:pieces], refs[pieces : pieces + 4]
    act, rows, weights, total = refs[pieces + 4 :]
    step = pl.program_id(0)
    units = weights_in[0].shape[0]

    @pl.when(step == 0)
    def _():
        rows[...] = jnp.zeros(rows.shape, jnp.bfloat16)
        total[...] = jnp.zeros(total.shape, jnp.float32)

    for offset, piece in zip(offsets, rows_in):
        rows[offset : offset + piece.shape[0], :] = piece[...]
    for number in range(4):
        weights[number * units : (number + 1) * units, :] = weights_in[number][...]
    total[...] += lax.dot_general(
        rows[...],
        weights[...],
        (((1,), (1,)), ((), ())),
        preferred_element_type=jnp.float32,
    )

    @pl.when(step == pl.num_programs(0) - 1)
    def _():
        gate = total[:, : 2 * units]
        up = total[:, 2 * units :]
        act[...] = (gate / (1.0 + jnp.exp(-gate)) * up).astype(jnp.bfloat16)


def hidden(row_pieces, weights):
    offsets, flat = [], []
    for number, parts in enumerate(row_pieces):
        offset = number * PADDED_CAP
        for part in parts:
            offsets.append(offset)
            flat.append(part)
            offset += part.shape[0]
    width = flat[0].shape[1]
    units = weights[0].shape[0]
    rows = len(row_pieces) * PADDED_CAP
    chunk = 1280
    weight_spec = pl.BlockSpec((units, chunk), lambda i: (0, i))
    return pl.pallas_call(
        functools.partial(hidden_kernel, tuple(offsets)),
        grid=(width // chunk,),
        out_shape=jax.ShapeDtypeStruct((rows, 2 * units), jnp.bfloat16),
        in_specs=[pl.BlockSpec((part.shape[0], chunk), lambda i: (0, i)) for part in flat]
        + [weight_spec] * 4,
        out_specs=pl.BlockSpec((rows, 2 * units), lambda i: (0, 0)),
        scratch_shapes=[
            pltpu.VMEM((rows, chunk), jnp.bfloat16),
            pltpu.VMEM((4 * units, chunk), jnp.bfloat16),
            pltpu.VMEM((rows, 4 * units), jnp.float32),
        ],
        compiler_params=pltpu.CompilerParams(vmem_limit_bytes=40 * MIB),
        cost_estimate=pl.CostEstimate(
            flops=8 * rows * width * units,
            bytes_accessed=2 * rows * width + 8 * width * units,
            transcendentals=2 * rows * units,
        ),
    )(*flat, *weights)


def down_kernel(places, act, down_own, down_other, out, weights, product):
    units = down_own.shape[0]
    pieces = out.shape[0]
    features = out.shape[3]
    weights[:units, :] = down_own[...]
    weights[units:, :] = down_other[...]
    product[...] = jnp.dot(act[...], weights[...], preferred_element_type=jnp.float32)
    for number in range(pieces):
        place = places[number]
        for part in range(out.shape[1]):
            out[place, part] = product[
                number * PADDED_CAP : number * PADDED_CAP + CAP,
                part * features : (part + 1) * features,
            ].astype(jnp.bfloat16)


def down(places, act, downs, parts):
    rows = act.shape[0]
    units, width = downs[0].shape
    pieces = rows // PADDED_CAP
    features = width // parts
    steps = 2
    weight_spec = pl.BlockSpec((units, width // steps), lambda i: (0, i))
    return pl.pallas_call(
        down_kernel,
        grid=(steps,),
        out_shape=jax.ShapeDtypeStruct((pieces, parts, CAP, features), jnp.bfloat16),
        in_specs=[SMEM, pl.BlockSpec(act.shape, lambda i: (0, 0)), weight_spec, weight_spec],
        out_specs=pl.BlockSpec((pieces, parts // steps, CAP, features), lambda i: (0, i, 0, 0)),
        scratch_shapes=[
            pltpu.VMEM((2 * units, width // steps), jnp.bfloat16),
            pltpu.VMEM((rows, width // steps), jnp.float32),
        ],
        compiler_params=pltpu.CompilerParams(vmem_limit_bytes=48 * MIB),
        cost_estimate=pl.CostEstimate(
            flops=4 * rows * width * units,
            bytes_accessed=2 * rows * width + 4 * width * units,
            transcendentals=0,
        ),
    )(places, act, *downs)


def collect_kernel(shares, table, out, merged):
    step = pl.program_id(0)
    sources, _, halves, rows, features = shares.shape
    total = jnp.zeros((rows, features), jnp.float32)
    for source in range(sources):
        for half in range(halves):
            total = total + shares[source, 0, half].astype(jnp.float32)
    spare = jnp.zeros((PADDED_CAP - rows, features), jnp.float32)
    merged[step] = jnp.concatenate([total, spare], axis=0).astype(jnp.bfloat16)

    @pl.when(step == pl.num_programs(0) - 1)
    def _():
        experts = merged.shape[0]
        stacked = merged[...].reshape(experts * PADDED_CAP, features)
        out[...] = lax.dot_general(
            stacked, table[...], (((0,), (0,)), ((), ())), preferred_element_type=jnp.float32
        ).astype(jnp.bfloat16)


def collect(shares, table):
    sources, experts, halves, rows, features = shares.shape
    tokens = table.shape[1]
    return pl.pallas_call(
        collect_kernel,
        grid=(experts,),
        out_shape=jax.ShapeDtypeStruct((features, tokens), jnp.bfloat16),
        in_specs=[
            pl.BlockSpec((sources, 1, halves, rows, features), lambda i: (0, i, 0, 0, 0)),
            pl.BlockSpec(table.shape, lambda i: (0, 0)),
        ],
        out_specs=pl.BlockSpec((features, tokens), lambda i: (0, 0)),
        scratch_shapes=[pltpu.VMEM((experts, PADDED_CAP, features), jnp.bfloat16)],
        compiler_params=pltpu.CompilerParams(vmem_limit_bytes=24 * MIB),
        cost_estimate=pl.CostEstimate(
            flops=2 * tokens * table.shape[0] * features,
            bytes_accessed=2 * shares.size + 2 * tokens * features,
            transcendentals=0,
        ),
    )(shares, table)


def shards(
    queries,
    common_keys,
    common_values,
    doc_ids,
    routes,
    residual,
    out_weight,
    norm_gain,
    gate_weight,
    up_weight,
    down_weight,
):
    ctx_size = lax.axis_size("ctx")
    exp_size = lax.axis_size("exp")
    chips = ctx_size // 2
    in_flight = exp_size // 2
    tokens = queries.shape[1]
    features = residual.shape[1]
    ctx = lax.axis_index("ctx")
    exp = lax.axis_index("exp")
    chip, core = ctx // 2, ctx % 2
    swap_cores = [(c, c ^ 1) for c in range(ctx_size)]

    own = jnp.concatenate([common_keys, common_values], axis=1)
    mine = [own] + [
        lax.ppermute(own, "ctx", [(c, c + 2 * s) for c in range(ctx_size - 2 * s)])
        for s in range(1, BACK + 1)
    ]
    theirs = [lax.ppermute(block, "ctx", swap_cores) for block in mine]

    blocks = mine + theirs
    query_docs = lax.dynamic_slice_in_dim(doc_ids, ctx * tokens, tokens)
    doc_numbers = jnp.arange(6, dtype=jnp.int32)
    starts = jnp.sum((doc_ids[None, :] < doc_numbers[:, None]).astype(jnp.int32), axis=1)
    low = jnp.sum(
        jnp.where(query_docs[None, :] == doc_numbers[:, None], starts[:, None], 0), axis=0
    )
    base = 2 * (chip - BACK)
    scalars = jnp.stack([low[0] // BLOCK - base, 2 * BACK + core, core, base, exp])
    scalars = scalars.astype(jnp.int32)

    product, table, slots_done = attend_slots(
        scalars,
        queries,
        routes.reshape(1, tokens),
        low.reshape(1, tokens),
        residual.T,
        out_weight,
        blocks,
        in_flight * PADDED_CAP,
    )
    shares = lax.all_to_all(
        product.reshape(exp_size, HALF, exp_size * features), "exp", 0, 0, tiled=True
    )
    first_attention, first_done = attend_first(
        scalars, queries, low.reshape(tokens, 1), blocks, after=(slots_done,)
    )
    gate, up, down_own = gate_weight[0].T, up_weight[0].T, down_weight[0]
    gate, up, down_own, _ = lax.optimization_barrier((gate, up, down_own, slots_done))
    gate_other, up_other, down_other = (
        lax.ppermute(weight, "ctx", swap_cores) for weight in (gate, up, down_own)
    )
    swapped = [weight[:16, :128] for weight in (gate_other, up_other, down_other)]
    normed = normalize(shares, norm_gain, after=(first_done, *swapped))

    pair = [(e, e ^ 1) for e in range(exp_size)]
    other = lax.ppermute(normed, "exp", pair)
    odd = exp % 2 == 1
    block = jnp.concatenate(
        [jnp.where(odd, other, normed), jnp.where(odd, normed, other)[: CAP - HALF]], axis=0
    )
    ring = chips // 2

    def beside(c, distance):
        chip_of, core_of = c // 2, c % 2
        place = (chip_of % ring + distance) % ring
        return (chip_of // ring * ring + place) * 2 + core_of

    right = [(c, beside(c, 1)) for c in range(ctx_size)]
    left = [(c, beside(c, -1)) for c in range(ctx_size)]
    across = [(c, (c + ctx_size // 2) % ctx_size) for c in range(ctx_size)]
    from_left = lax.ppermute(block, "ctx", right)
    from_right = lax.ppermute(block, "ctx", left)
    far = lax.ppermute(block, "ctx", across)
    opposite_top = lax.ppermute(from_left[:SPLIT], "ctx", right)
    opposite_rest = lax.ppermute(from_right[SPLIT:], "ctx", left)
    far_next, _, _ = lax.optimization_barrier((far, from_left, from_right))
    far_left = lax.ppermute(far_next, "ctx", right)
    far_right = lax.ppermute(far_next, "ctx", left)
    far_opposite_top = lax.ppermute(opposite_top, "ctx", across)
    far_opposite_rest = lax.ppermute(opposite_rest, "ctx", across)
    pieces = [
        (block,),
        (far,),
        (from_left,),
        (from_right,),
        (far_left,),
        (far_right,),
        (opposite_top, opposite_rest),
        (far_opposite_top, far_opposite_rest),
    ]
    row, along = chip // ring, chip % ring
    places = jnp.stack(
        [
            (row ^ z) * ring + (along + x) % ring
            for z, x in (
                (0, 0), (1, 0), (0, ring - 1), (0, 1), (1, ring - 1), (1, 1), (0, 2), (1, 2)
            )
        ]
    ).astype(jnp.int32)

    act = hidden(pieces, (gate, gate_other, up, up_other))
    partial = down(places, act, (down_own, down_other), exp_size)
    same_core = [
        [c * exp_size + e for c in range(k, ctx_size, 2) for e in range(exp_size)]
        for k in range(2)
    ]
    returned = lax.all_to_all(
        partial.reshape(chips * exp_size, CAP, features),
        ("ctx", "exp"),
        0,
        0,
        tiled=True,
        axis_index_groups=same_core,
    )
    expert_output = collect(returned.reshape(chips, in_flight, 2, CAP, features), table)
    return (first_attention, expert_output.T)


def solution(mesh):
    in_specs = (
        P(None, "ctx", "exp"),
        P("ctx", "exp"),
        P("ctx", "exp"),
        P(),
        P("ctx", None),
        P("ctx", "exp"),
        P("exp", None),
        P(),
        P("exp", None, "ctx"),
        P("exp", None, "ctx"),
        P("exp", "ctx", None),
    )
    out_specs = (P("ctx", "exp"), P("ctx", "exp"))
    return jax.shard_map(shards, mesh=mesh, in_specs=in_specs, out_specs=out_specs, check_vma=False)
```

```python
import functools

import jax
import jax.numpy as jnp
from jax import lax
from jax.experimental import pallas as pl
from jax.experimental.pallas import tpu as pltpu
from jax.sharding import PartitionSpec as P

QUERY_HEAD_COUNT = 40
SHARED_KV_HEADS = 8
HEAD_WIDTH = 128
CAP = 40
DOCS = 6

GROUP = QUERY_HEAD_COUNT // SHARED_KV_HEADS
BLOCK = 512
BACK = 4
KV_SLOTS = 2 * (BACK + 1)
PADDED_CAP = 48
HALF = PADDED_CAP // 2
SHARE = CAP // 2
SUB = 8
SPLIT = 16
MIB = 1 << 20
SLOTS_VMEM = 51
TILE = 256

big_negative = -1e30
norm_eps = 1e-06
log2e = 1.4426950408889634

VMEM = pl.BlockSpec(memory_space=pltpu.VMEM)
SMEM = pl.BlockSpec(memory_space=pltpu.SMEM)
ANY = pl.BlockSpec(memory_space=pl.ANY)
TOKEN = jax.ShapeDtypeStruct((8, 128), jnp.float32)


def fetch(sources, targets, done):
    copies = [
        pltpu.make_async_copy(source, target, done.at[number])
        for number, (source, target) in enumerate(zip(sources, targets))
    ]
    for copy in copies:
        copy.start()
    return copies


def span(scalars, low):
    chip, core = scalars[0] // 2, scalars[0] % 2
    base = 2 * (chip - BACK)
    first = jnp.min(low).astype(jnp.int32) // BLOCK - base
    return first, 2 * BACK + core, core, base


def flash(span_of, query, low, high, pairs, bias, highest, numer):
    first, last, core, base = span_of
    rows = query.shape[0]
    highest[...] = jnp.full(highest.shape, big_negative, jnp.float32)
    numer[...] = jnp.zeros(numer.shape, jnp.float32)
    scale = float(HEAD_WIDTH) ** (-0.5) * log2e
    ones = jnp.ones((BLOCK, HEAD_WIDTH), jnp.bfloat16)

    def step(at, carry):
        place = (base + at) * BLOCK + lax.broadcasted_iota(jnp.int32, (rows, BLOCK), 1)
        seen = (place >= low) & (place <= high)
        bias[...] = jnp.where(seen, 0.0, big_negative)
        slot = BACK - at // 2 + jnp.where(at % 2 == core, 0, BACK + 1)
        key_block = pairs[slot, :, :HEAD_WIDTH]
        value_block = jnp.concatenate([pairs[slot, :, HEAD_WIDTH:], ones], axis=1)
        tile = TILE if rows % TILE == 0 else rows
        for head in range(GROUP):
            for top in range(0, rows, tile):
                part = slice(top, top + tile)
                scores = lax.dot_general(
                    query[part, head * HEAD_WIDTH : (head + 1) * HEAD_WIDTH],
                    key_block,
                    (((1,), (1,)), ((), ())),
                    preferred_element_type=jnp.float32,
                )
                scores = scores + bias[part, :]
                old = highest[head, part]
                new = jnp.maximum(old, jnp.max(scores, axis=1, keepdims=True))
                probs = jnp.exp2((scores - new) * scale).astype(jnp.bfloat16)
                factor = jnp.exp2((old - new) * scale)
                highest[head, part] = new
                numer[head, part] = numer[head, part] * factor + jnp.dot(
                    probs, value_block, preferred_element_type=jnp.float32
                )
        return carry

    lax.fori_loop(first, last + 1, step, 0)


def store_heads(numer, out):
    for head in range(GROUP):
        summed = numer[head]
        out[:, head * HEAD_WIDTH : (head + 1) * HEAD_WIDTH] = (
            summed[:, :HEAD_WIDTH] / summed[:, HEAD_WIDTH:]
        ).astype(jnp.bfloat16)


def flash_scratch(rows, tokens, width):
    return [
        pltpu.VMEM((KV_SLOTS, BLOCK, 2 * HEAD_WIDTH), jnp.bfloat16),
        pltpu.VMEM((tokens, width), jnp.bfloat16),
        pltpu.VMEM((rows, BLOCK), jnp.float32),
        pltpu.VMEM((GROUP, rows, 1), jnp.float32),
        pltpu.VMEM((GROUP, rows, 2 * HEAD_WIDTH), jnp.float32),
        pltpu.SemaphoreType.DMA((KV_SLOTS + 4,)),
    ]


def flash_cost(rows, more_flops, more_bytes):
    typical = 6
    return pl.CostEstimate(
        flops=typical * GROUP * rows * BLOCK * HEAD_WIDTH * 8 + more_flops,
        bytes_accessed=KV_SLOTS * BLOCK * HEAD_WIDTH * 4 + more_bytes,
        transcendentals=typical * GROUP * rows * BLOCK,
    )


def first_kernel(scalars, queries, low, *refs):
    blocks = refs[:KV_SLOTS]
    out, token, pairs, query, bias, highest, numer, done = refs[-8:]
    token[...] = jnp.zeros(token.shape, jnp.float32)
    copies = fetch(
        [queries.at[0], *blocks], [query] + [pairs.at[n] for n in range(KV_SLOTS)], done
    )
    rows = query.shape[0]
    high = scalars[0] * BLOCK + lax.broadcasted_iota(jnp.int32, (rows, 1), 0)
    span_of = span(scalars, low[...].astype(jnp.float32))
    for copy in copies:
        copy.wait()
    flash(span_of, query, low[...], high, pairs, bias, highest, numer)
    store_heads(numer, out)


def attend_first(scalars, queries, low, blocks):
    _, rows, width = queries.shape
    return pl.pallas_call(
        first_kernel,
        out_shape=[jax.ShapeDtypeStruct((rows, width), jnp.bfloat16), TOKEN],
        in_specs=[SMEM, ANY, VMEM] + [ANY] * KV_SLOTS,
        out_specs=[VMEM, VMEM],
        scratch_shapes=flash_scratch(rows, rows, width),
        compiler_params=pltpu.CompilerParams(vmem_limit_bytes=58 * MIB),
        cost_estimate=flash_cost(rows, 0, 4 * rows * width),
    )(scalars, queries, low, *blocks)


def slots_kernel(scalars, queries, routes, docs, residual, weight, *refs):
    blocks = refs[:KV_SLOTS]
    out, table, low_out, pairs, query, bias, highest, numer, done = refs[KV_SLOTS : KV_SLOTS + 9]
    picked, mix, product, features_in, routes_in, docs_in = refs[KV_SLOTS + 9 :]
    copies = fetch(
        [routes, docs, queries.at[1], *blocks, residual],
        [routes_in, docs_in, query] + [pairs.at[n] for n in range(KV_SLOTS)] + [features_in],
        done,
    )
    rows, tokens = table.shape
    features = features_in.shape[0]
    copies[0].wait()
    copies[1].wait()
    across = tokens // docs_in.shape[1]
    own_docs = jnp.concatenate(
        [docs_in[pl.ds(scalars[0] * across + k, 1), :] for k in range(across)], axis=1
    )
    low = jnp.zeros((1, tokens), jnp.float32)
    for number in range(1, DOCS):
        before = jnp.where(docs_in[...] < number, 1.0, 0.0)
        before = jnp.sum(jnp.sum(before, axis=0, keepdims=True), axis=1, keepdims=True)
        low = jnp.where(own_docs == number, before, low)
    low_out[...] = low.astype(jnp.int32)
    span_of = span(scalars, low)
    route = routes_in[...]
    earlier = lax.broadcasted_iota(jnp.int32, (tokens, tokens), 0)
    earlier = earlier <= lax.broadcasted_iota(jnp.int32, (tokens, tokens), 1)
    named = lax.broadcasted_iota(jnp.int32, (16, tokens), 0) == route
    rank = jnp.dot(
        jnp.where(named, 1.0, 0.0).astype(jnp.bfloat16),
        jnp.where(earlier, 1.0, 0.0).astype(jnp.bfloat16),
        preferred_element_type=jnp.float32,
    )
    rank = rank.astype(jnp.int32) - 1
    number = lax.broadcasted_iota(jnp.int32, (PADDED_CAP, tokens), 0)
    for expert in range(rows // PADDED_CAP):
        placed = (rank[expert : expert + 1, :] == number) & (route == expert)
        table[expert * PADDED_CAP : (expert + 1) * PADDED_CAP, :] = jnp.where(
            placed, 1.0, 0.0
        ).astype(jnp.bfloat16)
    chosen = table[...]
    start = scalars[0] * BLOCK
    place = start + lax.broadcasted_iota(jnp.int32, (1, tokens), 1)
    held = chosen.astype(jnp.float32)
    slot_low = jnp.sum(held * low, axis=1, keepdims=True)
    slot_high = jnp.sum(held * place.astype(jnp.float32), axis=1, keepdims=True)
    slot_low = slot_low.astype(jnp.int32)
    slot_high = jnp.maximum(slot_high.astype(jnp.int32), start)
    copies[2].wait()
    picked[...] = jnp.dot(chosen, query[...], preferred_element_type=jnp.float32).astype(
        jnp.bfloat16
    )
    for copy in copies[3 : KV_SLOTS + 3]:
        copy.wait()
    flash(span_of, picked, slot_low, slot_high, pairs, bias, highest, numer)
    store_heads(numer, mix)
    for copy in copies[KV_SLOTS + 3 :]:
        copy.wait()
    product[...] = jnp.dot(mix[...], weight[...], preferred_element_type=jnp.float32)
    slot_resid = lax.dot_general(
        chosen, features_in[...], (((1,), (1,)), ((), ())), preferred_element_type=jnp.float32
    )
    for part in range(product.shape[1] // features):

        @pl.when(scalars[1] == part)
        def _():
            product[:, part * features : (part + 1) * features] += slot_resid

    width = product.shape[1]
    for part in range(out.shape[0]):
        base = part // 2 * PADDED_CAP + part % 2 * SHARE
        whole = SHARE // SUB
        for group in range(whole):
            at = base + group * SUB
            out[part, :, group * width : (group + 1) * width] = product[
                at : at + SUB, :
            ].astype(jnp.bfloat16)
        rest = product[base + whole * SUB : base + SHARE, :]
        rest = jnp.concatenate([rest[:, : width // 2], rest[:, width // 2 :]], axis=0)
        out[part, :, whole * width :] = rest.astype(jnp.bfloat16)


def attend_slots(scalars, queries, routes, docs, residual, weight, blocks, rows):
    _, tokens, width = queries.shape
    out_width = weight.shape[1]
    return pl.pallas_call(
        slots_kernel,
        out_shape=[
            jax.ShapeDtypeStruct(
                (2 * rows // PADDED_CAP, SUB, SHARE * out_width // SUB), jnp.bfloat16
            ),
            jax.ShapeDtypeStruct((rows, tokens), jnp.bfloat16),
            jax.ShapeDtypeStruct((1, tokens), jnp.int32),
        ],
        in_specs=[SMEM, ANY, ANY, ANY, ANY, VMEM] + [ANY] * KV_SLOTS,
        out_specs=[VMEM, VMEM, VMEM],
        scratch_shapes=flash_scratch(rows, tokens, width)
        + [
            pltpu.VMEM((rows, width), jnp.bfloat16),
            pltpu.VMEM((rows, width), jnp.bfloat16),
            pltpu.VMEM((rows, out_width), jnp.float32),
            pltpu.VMEM(residual.shape, jnp.bfloat16),
            pltpu.VMEM(routes.shape, jnp.int32),
            pltpu.VMEM(docs.shape, jnp.int32),
        ],
        compiler_params=pltpu.CompilerParams(vmem_limit_bytes=SLOTS_VMEM * MIB),
        cost_estimate=flash_cost(rows, 2 * rows * width * out_width, 2 * width * out_width),
    )(scalars, queries, routes, docs, residual, weight, *blocks)


def norm_kernel(shares, gain, *refs):
    out = refs[-1]
    total = shares[0].astype(jnp.float32)
    for number in range(1, shares.shape[0]):
        total = total + shares[number].astype(jnp.float32)
    rows, width = out.shape
    whole = SHARE // SUB
    groups = [total[:, group * width : (group + 1) * width] for group in range(whole)]
    rest = total[:, whole * width :]
    groups.append(jnp.concatenate([rest[: SUB // 2], rest[SUB // 2 :]], axis=1))
    groups.append(jnp.zeros((rows - SHARE, width), jnp.float32))
    state = jnp.concatenate(groups, axis=0)
    mean_square = jnp.mean(state * state, axis=1, keepdims=True)
    out[...] = (state * lax.rsqrt(mean_square + norm_eps) * gain[...]).astype(jnp.bfloat16)


def normalize(shares, norm_gain, after):
    count = shares.shape[0]
    rows, width = HALF, norm_gain.shape[0]
    return pl.pallas_call(
        norm_kernel,
        out_shape=jax.ShapeDtypeStruct((rows, width), jnp.bfloat16),
        in_specs=[VMEM, VMEM] + [VMEM] * len(after),
        out_specs=VMEM,
        compiler_params=pltpu.CompilerParams(vmem_limit_bytes=24 * MIB),
        cost_estimate=pl.CostEstimate(
            flops=count * rows * width * 3,
            bytes_accessed=(count + 1) * rows * width * 2,
            transcendentals=rows,
        ),
    )(shares, norm_gain.reshape(1, width), *after)


def hidden_kernel(offsets, *refs):
    pieces = len(offsets)
    rows_in, weights_in = refs[:pieces], refs[pieces : pieces + 4]
    act, rows, weights, total = refs[pieces + 4 :]
    step = pl.program_id(0)
    units = weights_in[0].shape[0]

    @pl.when(step == 0)
    def _():
        rows[...] = jnp.zeros(rows.shape, jnp.bfloat16)
        total[...] = jnp.zeros(total.shape, jnp.float32)

    for offset, piece in zip(offsets, rows_in):
        rows[offset : offset + piece.shape[0], :] = piece[...]
    for number in range(4):
        weights[number * units : (number + 1) * units, :] = weights_in[number][...]
    total[...] += lax.dot_general(
        rows[...],
        weights[...],
        (((1,), (1,)), ((), ())),
        preferred_element_type=jnp.float32,
    )

    @pl.when(step == pl.num_programs(0) - 1)
    def _():
        gate = total[:, : 2 * units]
        up = total[:, 2 * units :]
        act[...] = (gate / (1.0 + jnp.exp(-gate)) * up).astype(jnp.bfloat16)


def hidden(row_pieces, weights):
    offsets, flat = [], []
    for number, parts in enumerate(row_pieces):
        offset = number * PADDED_CAP
        for part in parts:
            offsets.append(offset)
            flat.append(part)
            offset += part.shape[0]
    width = flat[0].shape[1]
    units = weights[0].shape[0]
    rows = len(row_pieces) * PADDED_CAP
    chunk = 1280
    weight_spec = pl.BlockSpec((units, chunk), lambda i: (0, i))
    return pl.pallas_call(
        functools.partial(hidden_kernel, tuple(offsets)),
        grid=(width // chunk,),
        out_shape=jax.ShapeDtypeStruct((rows, 2 * units), jnp.bfloat16),
        in_specs=[pl.BlockSpec((part.shape[0], chunk), lambda i: (0, i)) for part in flat]
        + [weight_spec] * 4,
        out_specs=pl.BlockSpec((rows, 2 * units), lambda i: (0, 0)),
        scratch_shapes=[
            pltpu.VMEM((rows, chunk), jnp.bfloat16),
            pltpu.VMEM((4 * units, chunk), jnp.bfloat16),
            pltpu.VMEM((rows, 4 * units), jnp.float32),
        ],
        compiler_params=pltpu.CompilerParams(vmem_limit_bytes=40 * MIB),
        cost_estimate=pl.CostEstimate(
            flops=8 * rows * width * units,
            bytes_accessed=2 * rows * width + 8 * width * units,
            transcendentals=2 * rows * units,
        ),
    )(*flat, *weights)


def down_kernel(places, act, down_own, down_other, out, weights, product):
    units = down_own.shape[0]
    pieces, parts = out.shape[:2]
    features = product.shape[1] // parts
    weights[:units, :] = down_own[...]
    weights[units:, :] = down_other[...]
    product[...] = jnp.dot(act[...], weights[...], preferred_element_type=jnp.float32)
    for number in range(pieces):
        place = places[number]
        for part in range(parts):
            for group in range(CAP // SUB):
                at = number * PADDED_CAP + group * SUB
                out[place, part, :, group * features : (group + 1) * features] = product[
                    at : at + SUB, part * features : (part + 1) * features
                ].astype(jnp.bfloat16)


def down(places, act, downs, parts):
    rows = act.shape[0]
    units, width = downs[0].shape
    pieces = rows // PADDED_CAP
    packed = (SUB, CAP // SUB * (width // parts))
    steps = 2
    weight_spec = pl.BlockSpec((units, width // steps), lambda i: (0, i))
    return pl.pallas_call(
        down_kernel,
        grid=(steps,),
        out_shape=jax.ShapeDtypeStruct((pieces, parts, *packed), jnp.bfloat16),
        in_specs=[SMEM, pl.BlockSpec(act.shape, lambda i: (0, 0)), weight_spec, weight_spec],
        out_specs=pl.BlockSpec((pieces, parts // steps, *packed), lambda i: (0, i, 0, 0)),
        scratch_shapes=[
            pltpu.VMEM((2 * units, width // steps), jnp.bfloat16),
            pltpu.VMEM((rows, width // steps), jnp.float32),
        ],
        compiler_params=pltpu.CompilerParams(vmem_limit_bytes=48 * MIB),
        cost_estimate=pl.CostEstimate(
            flops=4 * rows * width * units,
            bytes_accessed=2 * rows * width + 4 * width * units,
            transcendentals=0,
        ),
    )(places, act, *downs)


def collect_kernel(shares, table, out, merged):
    step = pl.program_id(0)
    sources, _, halves, sub, packed = shares.shape
    features = merged.shape[2]
    total = jnp.zeros((sub, packed), jnp.float32)
    for source in range(sources):
        for half in range(halves):
            total = total + shares[source, 0, half].astype(jnp.float32)
    groups = [total[:, at : at + features] for at in range(0, packed, features)]
    groups.append(jnp.zeros((PADDED_CAP - CAP, features), jnp.float32))
    merged[step] = jnp.concatenate(groups, axis=0).astype(jnp.bfloat16)

    @pl.when(step == pl.num_programs(0) - 1)
    def _():
        experts = merged.shape[0]
        stacked = merged[...].reshape(experts * PADDED_CAP, features)
        out[...] = lax.dot_general(
            stacked, table[...], (((0,), (0,)), ((), ())), preferred_element_type=jnp.float32
        ).astype(jnp.bfloat16)


def collect(shares, table):
    sources, experts, halves, sub, packed = shares.shape
    features = packed * sub // CAP
    tokens = table.shape[1]
    return pl.pallas_call(
        collect_kernel,
        grid=(experts,),
        out_shape=jax.ShapeDtypeStruct((features, tokens), jnp.bfloat16),
        in_specs=[
            pl.BlockSpec((sources, 1, halves, sub, packed), lambda i: (0, i, 0, 0, 0)),
            pl.BlockSpec(table.shape, lambda i: (0, 0)),
        ],
        out_specs=pl.BlockSpec((features, tokens), lambda i: (0, 0)),
        scratch_shapes=[pltpu.VMEM((experts, PADDED_CAP, features), jnp.bfloat16)],
        compiler_params=pltpu.CompilerParams(vmem_limit_bytes=24 * MIB),
        cost_estimate=pl.CostEstimate(
            flops=2 * tokens * table.shape[0] * features,
            bytes_accessed=2 * shares.size + 2 * tokens * features,
            transcendentals=0,
        ),
    )(shares, table)


def shards(
    queries,
    common_keys,
    common_values,
    doc_ids,
    routes,
    residual,
    out_weight,
    norm_gain,
    gate_weight,
    up_weight,
    down_weight,
):
    ctx_size = lax.axis_size("ctx")
    exp_size = lax.axis_size("exp")
    chips = ctx_size // 2
    in_flight = exp_size // 2
    tokens = queries.shape[1]
    features = residual.shape[1]
    ctx = lax.axis_index("ctx")
    exp = lax.axis_index("exp")
    chip, core = ctx // 2, ctx % 2
    swap_cores = [(c, c ^ 1) for c in range(ctx_size)]

    own = jnp.concatenate([common_keys, common_values], axis=1)
    mine = [own] + [
        lax.ppermute(own, "ctx", [(c, c + 2 * s) for c in range(ctx_size - 2 * s)])
        for s in range(1, BACK + 1)
    ]
    theirs = [lax.ppermute(block, "ctx", swap_cores) for block in mine]

    blocks = mine + theirs
    scalars = jnp.stack([ctx, exp]).astype(jnp.int32)
    product, table, low = attend_slots(
        scalars,
        queries,
        routes.reshape(1, tokens),
        doc_ids.reshape(-1, 128),
        residual.T,
        out_weight,
        blocks,
        in_flight * PADDED_CAP,
    )
    shares = lax.all_to_all(product, "exp", 0, 0, tiled=True)
    first_attention, first_done = attend_first(scalars, queries, low.reshape(tokens, 1), blocks)
    gate, up, down_own = gate_weight[0].T, up_weight[0].T, down_weight[0]
    gate, up, down_own, _ = lax.optimization_barrier((gate, up, down_own, low))
    gate_other, up_other, down_other = (
        lax.ppermute(weight, "ctx", swap_cores) for weight in (gate, up, down_own)
    )
    swapped = [weight[:16, :128] for weight in (gate_other, up_other, down_other)]
    normed = normalize(shares, norm_gain, after=(first_done, *swapped))

    pair = [(e, e ^ 1) for e in range(exp_size)]
    other = lax.ppermute(normed, "exp", pair)
    odd = exp % 2 == 1
    block = jnp.concatenate(
        [jnp.where(odd, other, normed)[:SHARE], jnp.where(odd, normed, other)[:SHARE]], axis=0
    )
    ring = chips // 2

    def beside(c, distance):
        chip_of, core_of = c // 2, c % 2
        place = (chip_of % ring + distance) % ring
        return (chip_of // ring * ring + place) * 2 + core_of

    right = [(c, beside(c, 1)) for c in range(ctx_size)]
    left = [(c, beside(c, -1)) for c in range(ctx_size)]
    across = [(c, (c + ctx_size // 2) % ctx_size) for c in range(ctx_size)]
    from_left = lax.ppermute(block, "ctx", right)
    from_right = lax.ppermute(block, "ctx", left)
    far = lax.ppermute(block, "ctx", across)
    opposite_top = lax.ppermute(from_left[:SPLIT], "ctx", right)
    opposite_rest = lax.ppermute(from_right[SPLIT:], "ctx", left)
    far_next, _, _ = lax.optimization_barrier((far, from_left, from_right))
    far_left = lax.ppermute(far_next, "ctx", right)
    far_right = lax.ppermute(far_next, "ctx", left)
    far_opposite_top = lax.ppermute(opposite_top, "ctx", across)
    far_opposite_rest = lax.ppermute(opposite_rest, "ctx", across)
    pieces = [
        (block,),
        (far,),
        (from_left,),
        (from_right,),
        (far_left,),
        (far_right,),
        (opposite_top, opposite_rest),
        (far_opposite_top, far_opposite_rest),
    ]
    row, along = chip // ring, chip % ring
    places = jnp.stack(
        [
            (row ^ z) * ring + (along + x) % ring
            for z, x in (
                (0, 0), (1, 0), (0, ring - 1), (0, 1), (1, ring - 1), (1, 1), (0, 2), (1, 2)
            )
        ]
    ).astype(jnp.int32)

    act = hidden(pieces, (gate, gate_other, up, up_other))
    partial = down(places, act, (down_own, down_other), exp_size)
    same_core = [
        [c * exp_size + e for c in range(k, ctx_size, 2) for e in range(exp_size)]
        for k in range(2)
    ]
    returned = lax.all_to_all(
        partial.reshape(chips * exp_size, *partial.shape[2:]),
        ("ctx", "exp"),
        0,
        0,
        tiled=True,
        axis_index_groups=same_core,
    )
    expert_output = collect(returned.reshape(chips, in_flight, 2, *partial.shape[2:]), table)
    return (first_attention, expert_output.T)


def solution(mesh):
    in_specs = (
        P(None, "ctx", "exp"),
        P("ctx", "exp"),
        P("ctx", "exp"),
        P(),
        P("ctx", None),
        P("ctx", "exp"),
        P("exp", None),
        P(),
        P("exp", None, "ctx"),
        P("exp", None, "ctx"),
        P("exp", "ctx", None),
    )
    out_specs = (P("ctx", "exp"), P("ctx", "exp"))
    return jax.shard_map(shards, mesh=mesh, in_specs=in_specs, out_specs=out_specs, check_vma=False)
```

```python
import functools

import jax
import jax.numpy as jnp
from jax import lax
from jax.experimental import pallas as pl
from jax.experimental.pallas import tpu as pltpu
from jax.sharding import PartitionSpec as P

QUERY_HEAD_COUNT = 40
SHARED_KV_HEADS = 8
HEAD_WIDTH = 128
CAP = 40
DOCS = 6

GROUP = QUERY_HEAD_COUNT // SHARED_KV_HEADS
BLOCK = 512
BACK = 4
KV_SLOTS = 2 * (BACK + 1)
PADDED_CAP = 48
HALF = PADDED_CAP // 2
SHARE = CAP // 2
SUB = 8
SPLIT = 16
MIB = 1 << 20
SLOTS_VMEM = 51
TILE = 256

big_negative = -1e30
norm_eps = 1e-06
log2e = 1.4426950408889634

VMEM = pl.BlockSpec(memory_space=pltpu.VMEM)
SMEM = pl.BlockSpec(memory_space=pltpu.SMEM)
ANY = pl.BlockSpec(memory_space=pl.ANY)
TOKEN = jax.ShapeDtypeStruct((8, 128), jnp.float32)


def fetch(sources, targets, done):
    copies = [
        pltpu.make_async_copy(source, target, done.at[number])
        for number, (source, target) in enumerate(zip(sources, targets))
    ]
    for copy in copies:
        copy.start()
    return copies


def span(scalars, low):
    chip, core = scalars[0] // 2, scalars[0] % 2
    base = 2 * (chip - BACK)
    first = jnp.min(low).astype(jnp.int32) // BLOCK - base
    return first, 2 * BACK + core, core, base


def flash(span_of, query, low, high, pairs, bias, highest, numer):
    first, last, core, base = span_of
    rows = query.shape[0]
    highest[...] = jnp.full(highest.shape, big_negative, jnp.float32)
    numer[...] = jnp.zeros(numer.shape, jnp.float32)
    scale = float(HEAD_WIDTH) ** (-0.5) * log2e
    ones = jnp.ones((BLOCK, HEAD_WIDTH), jnp.bfloat16)
    tile = TILE if rows % TILE == 0 else rows
    tops = range(0, rows, tile)

    def hide(at):
        place = (base + at) * BLOCK + lax.broadcasted_iota(jnp.int32, (rows, BLOCK), 1)
        seen = (place >= low) & (place <= high)
        bias[...] = jnp.where(seen, 0.0, big_negative)
        return BACK - at // 2 + jnp.where(at % 2 == core, 0, BACK + 1)

    def score(head, part, key_block):
        scores = lax.dot_general(
            query[part, head * HEAD_WIDTH : (head + 1) * HEAD_WIDTH],
            key_block,
            (((1,), (1,)), ((), ())),
            preferred_element_type=jnp.float32,
        )
        return scores + bias[part, :]

    def find_highest(at, carry):
        key_block = pairs[hide(at), :, :HEAD_WIDTH]
        for head in range(GROUP):
            for top in tops:
                part = slice(top, top + tile)
                scores = score(head, part, key_block)
                most = highest[head, part]
                for lane in range(0, BLOCK, HEAD_WIDTH):
                    most = jnp.maximum(most, scores[:, lane : lane + HEAD_WIDTH])
                highest[head, part] = most
        return carry

    lax.fori_loop(first, last + 1, find_highest, 0)
    for head in range(GROUP):
        most = jnp.max(highest[head], axis=1, keepdims=True)
        highest[head] = jnp.broadcast_to(most, (rows, HEAD_WIDTH))

    def add_block(at, carry):
        slot = hide(at)
        key_block = pairs[slot, :, :HEAD_WIDTH]
        value_block = jnp.concatenate([pairs[slot, :, HEAD_WIDTH:], ones], axis=1)
        for head in range(GROUP):
            for top in tops:
                part = slice(top, top + tile)
                most = jnp.concatenate([highest[head, part]] * (BLOCK // HEAD_WIDTH), axis=1)
                probs = jnp.exp2((score(head, part, key_block) - most) * scale)
                numer[head, part] += jnp.dot(
                    probs.astype(jnp.bfloat16), value_block, preferred_element_type=jnp.float32
                )
        return carry

    lax.fori_loop(first, last + 1, add_block, 0)


def store_heads(numer, out):
    for head in range(GROUP):
        summed = numer[head]
        out[:, head * HEAD_WIDTH : (head + 1) * HEAD_WIDTH] = (
            summed[:, :HEAD_WIDTH] / summed[:, HEAD_WIDTH:]
        ).astype(jnp.bfloat16)


def flash_scratch(rows, tokens, width):
    return [
        pltpu.VMEM((KV_SLOTS, BLOCK, 2 * HEAD_WIDTH), jnp.bfloat16),
        pltpu.VMEM((tokens, width), jnp.bfloat16),
        pltpu.VMEM((rows, BLOCK), jnp.float32),
        pltpu.VMEM((GROUP, rows, HEAD_WIDTH), jnp.float32),
        pltpu.VMEM((GROUP, rows, 2 * HEAD_WIDTH), jnp.float32),
        pltpu.SemaphoreType.DMA((KV_SLOTS + 4,)),
    ]


def flash_cost(rows, more_flops, more_bytes):
    typical = 6
    return pl.CostEstimate(
        flops=typical * GROUP * rows * BLOCK * HEAD_WIDTH * 8 + more_flops,
        bytes_accessed=KV_SLOTS * BLOCK * HEAD_WIDTH * 4 + more_bytes,
        transcendentals=typical * GROUP * rows * BLOCK,
    )


def first_kernel(scalars, queries, low, *refs):
    blocks = refs[:KV_SLOTS]
    out, token, pairs, query, bias, highest, numer, done = refs[-8:]
    token[...] = jnp.zeros(token.shape, jnp.float32)
    copies = fetch(
        [queries.at[0], *blocks], [query] + [pairs.at[n] for n in range(KV_SLOTS)], done
    )
    rows = query.shape[0]
    high = scalars[0] * BLOCK + lax.broadcasted_iota(jnp.int32, (rows, 1), 0)
    span_of = span(scalars, low[...].astype(jnp.float32))
    for copy in copies:
        copy.wait()
    flash(span_of, query, low[...], high, pairs, bias, highest, numer)
    store_heads(numer, out)


def attend_first(scalars, queries, low, blocks):
    _, rows, width = queries.shape
    return pl.pallas_call(
        first_kernel,
        out_shape=[jax.ShapeDtypeStruct((rows, width), jnp.bfloat16), TOKEN],
        in_specs=[SMEM, ANY, VMEM] + [ANY] * KV_SLOTS,
        out_specs=[VMEM, VMEM],
        scratch_shapes=flash_scratch(rows, rows, width),
        compiler_params=pltpu.CompilerParams(vmem_limit_bytes=58 * MIB),
        cost_estimate=flash_cost(rows, 0, 4 * rows * width),
    )(scalars, queries, low, *blocks)


def slots_kernel(scalars, queries, routes, docs, residual, weight, *refs):
    blocks = refs[:KV_SLOTS]
    out, table, low_out, pairs, query, bias, highest, numer, done = refs[KV_SLOTS : KV_SLOTS + 9]
    picked, mix, product, features_in, routes_in, docs_in = refs[KV_SLOTS + 9 :]
    copies = fetch(
        [routes, docs, queries.at[1], *blocks, residual],
        [routes_in, docs_in, query] + [pairs.at[n] for n in range(KV_SLOTS)] + [features_in],
        done,
    )
    rows, tokens = table.shape
    features = features_in.shape[0]
    copies[0].wait()
    copies[1].wait()
    across = tokens // docs_in.shape[1]
    own_docs = jnp.concatenate(
        [docs_in[pl.ds(scalars[0] * across + k, 1), :] for k in range(across)], axis=1
    )
    low = jnp.zeros((1, tokens), jnp.float32)
    for number in range(1, DOCS):
        before = jnp.where(docs_in[...] < number, 1.0, 0.0)
        before = jnp.sum(jnp.sum(before, axis=0, keepdims=True), axis=1, keepdims=True)
        low = jnp.where(own_docs == number, before, low)
    low_out[...] = low.astype(jnp.int32)
    span_of = span(scalars, low)
    route = routes_in[...]
    earlier = lax.broadcasted_iota(jnp.int32, (tokens, tokens), 0)
    earlier = earlier <= lax.broadcasted_iota(jnp.int32, (tokens, tokens), 1)
    named = lax.broadcasted_iota(jnp.int32, (16, tokens), 0) == route
    rank = jnp.dot(
        jnp.where(named, 1.0, 0.0).astype(jnp.bfloat16),
        jnp.where(earlier, 1.0, 0.0).astype(jnp.bfloat16),
        preferred_element_type=jnp.float32,
    )
    rank = rank.astype(jnp.int32) - 1
    number = lax.broadcasted_iota(jnp.int32, (PADDED_CAP, tokens), 0)
    for expert in range(rows // PADDED_CAP):
        placed = (rank[expert : expert + 1, :] == number) & (route == expert)
        table[expert * PADDED_CAP : (expert + 1) * PADDED_CAP, :] = jnp.where(
            placed, 1.0, 0.0
        ).astype(jnp.bfloat16)
    chosen = table[...]
    start = scalars[0] * BLOCK
    place = start + lax.broadcasted_iota(jnp.int32, (1, tokens), 1)
    held = chosen.astype(jnp.float32)
    slot_low = jnp.sum(held * low, axis=1, keepdims=True)
    slot_high = jnp.sum(held * place.astype(jnp.float32), axis=1, keepdims=True)
    slot_low = slot_low.astype(jnp.int32)
    slot_high = jnp.maximum(slot_high.astype(jnp.int32), start)
    copies[2].wait()
    picked[...] = jnp.dot(chosen, query[...], preferred_element_type=jnp.float32).astype(
        jnp.bfloat16
    )
    for copy in copies[3 : KV_SLOTS + 3]:
        copy.wait()
    flash(span_of, picked, slot_low, slot_high, pairs, bias, highest, numer)
    store_heads(numer, mix)
    for copy in copies[KV_SLOTS + 3 :]:
        copy.wait()
    product[...] = jnp.dot(mix[...], weight[...], preferred_element_type=jnp.float32)
    slot_resid = lax.dot_general(
        chosen, features_in[...], (((1,), (1,)), ((), ())), preferred_element_type=jnp.float32
    )
    for part in range(product.shape[1] // features):

        @pl.when(scalars[1] == part)
        def _():
            product[:, part * features : (part + 1) * features] += slot_resid

    width = product.shape[1]
    for part in range(out.shape[0]):
        base = part // 2 * PADDED_CAP + part % 2 * SHARE
        whole = SHARE // SUB
        for group in range(whole):
            at = base + group * SUB
            out[part, :, group * width : (group + 1) * width] = product[
                at : at + SUB, :
            ].astype(jnp.bfloat16)
        rest = product[base + whole * SUB : base + SHARE, :]
        rest = jnp.concatenate([rest[:, : width // 2], rest[:, width // 2 :]], axis=0)
        out[part, :, whole * width :] = rest.astype(jnp.bfloat16)


def attend_slots(scalars, queries, routes, docs, residual, weight, blocks, rows):
    _, tokens, width = queries.shape
    out_width = weight.shape[1]
    return pl.pallas_call(
        slots_kernel,
        out_shape=[
            jax.ShapeDtypeStruct(
                (2 * rows // PADDED_CAP, SUB, SHARE * out_width // SUB), jnp.bfloat16
            ),
            jax.ShapeDtypeStruct((rows, tokens), jnp.bfloat16),
            jax.ShapeDtypeStruct((1, tokens), jnp.int32),
        ],
        in_specs=[SMEM, ANY, ANY, ANY, ANY, VMEM] + [ANY] * KV_SLOTS,
        out_specs=[VMEM, VMEM, VMEM],
        scratch_shapes=flash_scratch(rows, tokens, width)
        + [
            pltpu.VMEM((rows, width), jnp.bfloat16),
            pltpu.VMEM((rows, width), jnp.bfloat16),
            pltpu.VMEM((rows, out_width), jnp.float32),
            pltpu.VMEM(residual.shape, jnp.bfloat16),
            pltpu.VMEM(routes.shape, jnp.int32),
            pltpu.VMEM(docs.shape, jnp.int32),
        ],
        compiler_params=pltpu.CompilerParams(vmem_limit_bytes=SLOTS_VMEM * MIB),
        cost_estimate=flash_cost(rows, 2 * rows * width * out_width, 2 * width * out_width),
    )(scalars, queries, routes, docs, residual, weight, *blocks)


def norm_kernel(shares, gain, *refs):
    out = refs[-1]
    total = shares[0].astype(jnp.float32)
    for number in range(1, shares.shape[0]):
        total = total + shares[number].astype(jnp.float32)
    rows, width = out.shape
    whole = SHARE // SUB
    groups = [total[:, group * width : (group + 1) * width] for group in range(whole)]
    rest = total[:, whole * width :]
    groups.append(jnp.concatenate([rest[: SUB // 2], rest[SUB // 2 :]], axis=1))
    groups.append(jnp.zeros((rows - SHARE, width), jnp.float32))
    state = jnp.concatenate(groups, axis=0)
    mean_square = jnp.mean(state * state, axis=1, keepdims=True)
    out[...] = (state * lax.rsqrt(mean_square + norm_eps) * gain[...]).astype(jnp.bfloat16)


def normalize(shares, norm_gain, after):
    count = shares.shape[0]
    rows, width = HALF, norm_gain.shape[0]
    return pl.pallas_call(
        norm_kernel,
        out_shape=jax.ShapeDtypeStruct((rows, width), jnp.bfloat16),
        in_specs=[VMEM, VMEM] + [VMEM] * len(after),
        out_specs=VMEM,
        compiler_params=pltpu.CompilerParams(vmem_limit_bytes=24 * MIB),
        cost_estimate=pl.CostEstimate(
            flops=count * rows * width * 3,
            bytes_accessed=(count + 1) * rows * width * 2,
            transcendentals=rows,
        ),
    )(shares, norm_gain.reshape(1, width), *after)


def hidden_kernel(offsets, *refs):
    pieces = len(offsets)
    rows_in, weights_in = refs[:pieces], refs[pieces : pieces + 4]
    act, rows, weights, total = refs[pieces + 4 :]
    step = pl.program_id(0)
    units = weights_in[0].shape[0]

    @pl.when(step == 0)
    def _():
        rows[...] = jnp.zeros(rows.shape, jnp.bfloat16)
        total[...] = jnp.zeros(total.shape, jnp.float32)

    for offset, piece in zip(offsets, rows_in):
        rows[offset : offset + piece.shape[0], :] = piece[...]
    for number in range(4):
        weights[number * units : (number + 1) * units, :] = weights_in[number][...]
    total[...] += lax.dot_general(
        rows[...],
        weights[...],
        (((1,), (1,)), ((), ())),
        preferred_element_type=jnp.float32,
    )

    @pl.when(step == pl.num_programs(0) - 1)
    def _():
        gate = total[:, : 2 * units]
        up = total[:, 2 * units :]
        act[...] = (gate / (1.0 + jnp.exp(-gate)) * up).astype(jnp.bfloat16)


def hidden(row_pieces, weights):
    offsets, flat = [], []
    for number, parts in enumerate(row_pieces):
        offset = number * PADDED_CAP
        for part in parts:
            offsets.append(offset)
            flat.append(part)
            offset += part.shape[0]
    width = flat[0].shape[1]
    units = weights[0].shape[0]
    rows = len(row_pieces) * PADDED_CAP
    chunk = 1280
    weight_spec = pl.BlockSpec((units, chunk), lambda i: (0, i))
    return pl.pallas_call(
        functools.partial(hidden_kernel, tuple(offsets)),
        grid=(width // chunk,),
        out_shape=jax.ShapeDtypeStruct((rows, 2 * units), jnp.bfloat16),
        in_specs=[pl.BlockSpec((part.shape[0], chunk), lambda i: (0, i)) for part in flat]
        + [weight_spec] * 4,
        out_specs=pl.BlockSpec((rows, 2 * units), lambda i: (0, 0)),
        scratch_shapes=[
            pltpu.VMEM((rows, chunk), jnp.bfloat16),
            pltpu.VMEM((4 * units, chunk), jnp.bfloat16),
            pltpu.VMEM((rows, 4 * units), jnp.float32),
        ],
        compiler_params=pltpu.CompilerParams(vmem_limit_bytes=40 * MIB),
        cost_estimate=pl.CostEstimate(
            flops=8 * rows * width * units,
            bytes_accessed=2 * rows * width + 8 * width * units,
            transcendentals=2 * rows * units,
        ),
    )(*flat, *weights)


def down_kernel(places, act, down_own, down_other, out, weights, product):
    units = down_own.shape[0]
    pieces, parts = out.shape[:2]
    features = product.shape[1] // parts
    weights[:units, :] = down_own[...]
    weights[units:, :] = down_other[...]
    product[...] = jnp.dot(act[...], weights[...], preferred_element_type=jnp.float32)
    for number in range(pieces):
        place = places[number]
        for part in range(parts):
            for group in range(CAP // SUB):
                at = number * PADDED_CAP + group * SUB
                out[place, part, :, group * features : (group + 1) * features] = product[
                    at : at + SUB, part * features : (part + 1) * features
                ].astype(jnp.bfloat16)


def down(places, act, downs, parts):
    rows = act.shape[0]
    units, width = downs[0].shape
    pieces = rows // PADDED_CAP
    packed = (SUB, CAP // SUB * (width // parts))
    steps = 2
    weight_spec = pl.BlockSpec((units, width // steps), lambda i: (0, i))
    return pl.pallas_call(
        down_kernel,
        grid=(steps,),
        out_shape=jax.ShapeDtypeStruct((pieces, parts, *packed), jnp.bfloat16),
        in_specs=[SMEM, pl.BlockSpec(act.shape, lambda i: (0, 0)), weight_spec, weight_spec],
        out_specs=pl.BlockSpec((pieces, parts // steps, *packed), lambda i: (0, i, 0, 0)),
        scratch_shapes=[
            pltpu.VMEM((2 * units, width // steps), jnp.bfloat16),
            pltpu.VMEM((rows, width // steps), jnp.float32),
        ],
        compiler_params=pltpu.CompilerParams(vmem_limit_bytes=48 * MIB),
        cost_estimate=pl.CostEstimate(
            flops=4 * rows * width * units,
            bytes_accessed=2 * rows * width + 4 * width * units,
            transcendentals=0,
        ),
    )(places, act, *downs)


def collect_kernel(shares, table, out, merged):
    step = pl.program_id(0)
    sources, _, halves, sub, packed = shares.shape
    features = merged.shape[2]
    total = jnp.zeros((sub, packed), jnp.float32)
    for source in range(sources):
        for half in range(halves):
            total = total + shares[source, 0, half].astype(jnp.float32)
    groups = [total[:, at : at + features] for at in range(0, packed, features)]
    groups.append(jnp.zeros((PADDED_CAP - CAP, features), jnp.float32))
    merged[step] = jnp.concatenate(groups, axis=0).astype(jnp.bfloat16)

    @pl.when(step == pl.num_programs(0) - 1)
    def _():
        experts = merged.shape[0]
        stacked = merged[...].reshape(experts * PADDED_CAP, features)
        out[...] = lax.dot_general(
            stacked, table[...], (((0,), (0,)), ((), ())), preferred_element_type=jnp.float32
        ).astype(jnp.bfloat16)


def collect(shares, table):
    sources, experts, halves, sub, packed = shares.shape
    features = packed * sub // CAP
    tokens = table.shape[1]
    return pl.pallas_call(
        collect_kernel,
        grid=(experts,),
        out_shape=jax.ShapeDtypeStruct((features, tokens), jnp.bfloat16),
        in_specs=[
            pl.BlockSpec((sources, 1, halves, sub, packed), lambda i: (0, i, 0, 0, 0)),
            pl.BlockSpec(table.shape, lambda i: (0, 0)),
        ],
        out_specs=pl.BlockSpec((features, tokens), lambda i: (0, 0)),
        scratch_shapes=[pltpu.VMEM((experts, PADDED_CAP, features), jnp.bfloat16)],
        compiler_params=pltpu.CompilerParams(vmem_limit_bytes=24 * MIB),
        cost_estimate=pl.CostEstimate(
            flops=2 * tokens * table.shape[0] * features,
            bytes_accessed=2 * shares.size + 2 * tokens * features,
            transcendentals=0,
        ),
    )(shares, table)


def shards(
    queries,
    common_keys,
    common_values,
    doc_ids,
    routes,
    residual,
    out_weight,
    norm_gain,
    gate_weight,
    up_weight,
    down_weight,
):
    ctx_size = lax.axis_size("ctx")
    exp_size = lax.axis_size("exp")
    chips = ctx_size // 2
    in_flight = exp_size // 2
    tokens = queries.shape[1]
    features = residual.shape[1]
    ctx = lax.axis_index("ctx")
    exp = lax.axis_index("exp")
    chip, core = ctx // 2, ctx % 2
    swap_cores = [(c, c ^ 1) for c in range(ctx_size)]

    own = jnp.concatenate([common_keys, common_values], axis=1)
    mine = [own] + [
        lax.ppermute(own, "ctx", [(c, c + 2 * s) for c in range(ctx_size - 2 * s)])
        for s in range(1, BACK + 1)
    ]
    theirs = [lax.ppermute(block, "ctx", swap_cores) for block in mine]

    blocks = mine + theirs
    scalars = jnp.stack([ctx, exp]).astype(jnp.int32)
    product, table, low = attend_slots(
        scalars,
        queries,
        routes.reshape(1, tokens),
        doc_ids.reshape(-1, 128),
        residual.T,
        out_weight,
        blocks,
        in_flight * PADDED_CAP,
    )
    shares = lax.all_to_all(product, "exp", 0, 0, tiled=True)
    first_attention, first_done = attend_first(scalars, queries, low.reshape(tokens, 1), blocks)
    gate, up, down_own = gate_weight[0].T, up_weight[0].T, down_weight[0]
    gate, up, down_own, _ = lax.optimization_barrier((gate, up, down_own, low))
    gate_other, up_other, down_other = (
        lax.ppermute(weight, "ctx", swap_cores) for weight in (gate, up, down_own)
    )
    swapped = gate_other[:8, :128] + up_other[:8, :128] + down_other[:8, :128]
    normed = normalize(shares, norm_gain, after=(first_done + swapped.astype(jnp.float32),))

    pair = [(e, e ^ 1) for e in range(exp_size)]
    other = lax.ppermute(normed, "exp", pair)
    odd = exp % 2 == 1
    block = jnp.concatenate(
        [jnp.where(odd, other, normed)[:SHARE], jnp.where(odd, normed, other)[:SHARE]], axis=0
    )
    ring = chips // 2

    def beside(c, distance):
        chip_of, core_of = c // 2, c % 2
        place = (chip_of % ring + distance) % ring
        return (chip_of // ring * ring + place) * 2 + core_of

    right = [(c, beside(c, 1)) for c in range(ctx_size)]
    left = [(c, beside(c, -1)) for c in range(ctx_size)]
    across = [(c, (c + ctx_size // 2) % ctx_size) for c in range(ctx_size)]
    from_left = lax.ppermute(block, "ctx", right)
    from_right = lax.ppermute(block, "ctx", left)
    far = lax.ppermute(block, "ctx", across)
    opposite_top = lax.ppermute(from_left[:SPLIT], "ctx", right)
    opposite_rest = lax.ppermute(from_right[SPLIT:], "ctx", left)
    far_next, _, _ = lax.optimization_barrier((far, from_left, from_right))
    far_left = lax.ppermute(far_next, "ctx", right)
    far_right = lax.ppermute(far_next, "ctx", left)
    far_opposite_top = lax.ppermute(opposite_top, "ctx", across)
    far_opposite_rest = lax.ppermute(opposite_rest, "ctx", across)
    pieces = [
        (block,),
        (far,),
        (from_left,),
        (from_right,),
        (far_left,),
        (far_right,),
        (opposite_top, opposite_rest),
        (far_opposite_top, far_opposite_rest),
    ]
    row, along = chip // ring, chip % ring
    places = jnp.stack(
        [
            (row ^ z) * ring + (along + x) % ring
            for z, x in (
                (0, 0), (1, 0), (0, ring - 1), (0, 1), (1, ring - 1), (1, 1), (0, 2), (1, 2)
            )
        ]
    ).astype(jnp.int32)

    act = hidden(pieces, (gate, gate_other, up, up_other))
    partial = down(places, act, (down_own, down_other), exp_size)
    same_core = [
        [c * exp_size + e for c in range(k, ctx_size, 2) for e in range(exp_size)]
        for k in range(2)
    ]
    returned = lax.all_to_all(
        partial.reshape(chips * exp_size, *partial.shape[2:]),
        ("ctx", "exp"),
        0,
        0,
        tiled=True,
        axis_index_groups=same_core,
    )
    expert_output = collect(returned.reshape(chips, in_flight, 2, *partial.shape[2:]), table)
    return (first_attention, expert_output.T)


def solution(mesh):
    in_specs = (
        P(None, "ctx", "exp"),
        P("ctx", "exp"),
        P("ctx", "exp"),
        P(),
        P("ctx", None),
        P("ctx", "exp"),
        P("exp", None),
        P(),
        P("exp", None, "ctx"),
        P("exp", None, "ctx"),
        P("exp", "ctx", None),
    )
    out_specs = (P("ctx", "exp"), P("ctx", "exp"))
    return jax.shard_map(shards, mesh=mesh, in_specs=in_specs, out_specs=out_specs, check_vma=False)
```

```python
import functools

import jax
import jax.numpy as jnp
from jax import lax
from jax.experimental import pallas as pl
from jax.experimental.pallas import tpu as pltpu
from jax.sharding import PartitionSpec as P

QUERY_HEAD_COUNT = 40
SHARED_KV_HEADS = 8
HEAD_WIDTH = 128
CAP = 40
DOCS = 6

GROUP = QUERY_HEAD_COUNT // SHARED_KV_HEADS
BLOCK = 512
BACK = 4
KV_SLOTS = 2 * (BACK + 1)
PADDED_CAP = 48
HALF = PADDED_CAP // 2
SHARE = CAP // 2
SUB = 8
SPLIT = 16
MIB = 1 << 20
SLOTS_VMEM = 51
TILE = 256

big_negative = -1e30
norm_eps = 1e-06
log2e = 1.4426950408889634

VMEM = pl.BlockSpec(memory_space=pltpu.VMEM)
SMEM = pl.BlockSpec(memory_space=pltpu.SMEM)
ANY = pl.BlockSpec(memory_space=pl.ANY)
TOKEN = jax.ShapeDtypeStruct((8, 128), jnp.float32)


def fetch(sources, targets, done):
    copies = [
        pltpu.make_async_copy(source, target, done.at[number])
        for number, (source, target) in enumerate(zip(sources, targets))
    ]
    for copy in copies:
        copy.start()
    return copies


def span(scalars, low):
    chip, core = scalars[0] // 2, scalars[0] % 2
    base = 2 * (chip - BACK)
    first = jnp.min(low).astype(jnp.int32) // BLOCK - base
    return first, 2 * BACK + core, core, base


def flash(span_of, query, low, high, pairs, bias, highest, numer):
    first, last, core, base = span_of
    rows = query.shape[0]
    highest[...] = jnp.full(highest.shape, big_negative, jnp.float32)
    numer[...] = jnp.zeros(numer.shape, jnp.float32)
    scale = float(HEAD_WIDTH) ** (-0.5) * log2e
    ones = jnp.ones((BLOCK, HEAD_WIDTH), jnp.bfloat16)
    tile = TILE if rows % TILE == 0 else rows
    tops = range(0, rows, tile)

    def hide(at):
        place = (base + at) * BLOCK + lax.broadcasted_iota(jnp.int32, (rows, BLOCK), 1)
        seen = (place >= low) & (place <= high)
        bias[...] = jnp.where(seen, 0.0, big_negative)
        return BACK - at // 2 + jnp.where(at % 2 == core, 0, BACK + 1)

    def score(head, part, key_block):
        scores = lax.dot_general(
            query[part, head * HEAD_WIDTH : (head + 1) * HEAD_WIDTH],
            key_block,
            (((1,), (1,)), ((), ())),
            preferred_element_type=jnp.float32,
        )
        return scores + bias[part, :]

    def find_highest(at, carry):
        key_block = pairs[hide(at), :, :HEAD_WIDTH]
        for head in range(GROUP):
            for top in tops:
                part = slice(top, top + tile)
                scores = score(head, part, key_block)
                most = highest[head, part]
                for lane in range(0, BLOCK, HEAD_WIDTH):
                    most = jnp.maximum(most, scores[:, lane : lane + HEAD_WIDTH])
                highest[head, part] = most
        return carry

    lax.fori_loop(first, last + 1, find_highest, 0)
    for head in range(GROUP):
        most = jnp.max(highest[head], axis=1, keepdims=True)
        highest[head] = jnp.broadcast_to(most, (rows, HEAD_WIDTH))

    def add_block(at, carry):
        slot = hide(at)
        key_block = pairs[slot, :, :HEAD_WIDTH]
        value_block = jnp.concatenate([pairs[slot, :, HEAD_WIDTH:], ones], axis=1)
        for head in range(GROUP):
            for top in tops:
                part = slice(top, top + tile)
                most = jnp.concatenate([highest[head, part]] * (BLOCK // HEAD_WIDTH), axis=1)
                probs = jnp.exp2((score(head, part, key_block) - most) * scale)
                numer[head, part] += jnp.dot(
                    probs.astype(jnp.bfloat16), value_block, preferred_element_type=jnp.float32
                )
        return carry

    lax.fori_loop(first, last + 1, add_block, 0)


def store_heads(numer, out):
    for head in range(GROUP):
        summed = numer[head]
        out[:, head * HEAD_WIDTH : (head + 1) * HEAD_WIDTH] = (
            summed[:, :HEAD_WIDTH] / summed[:, HEAD_WIDTH:]
        ).astype(jnp.bfloat16)


def flash_scratch(rows, tokens, width):
    return [
        pltpu.VMEM((KV_SLOTS, BLOCK, 2 * HEAD_WIDTH), jnp.bfloat16),
        pltpu.VMEM((tokens, width), jnp.bfloat16),
        pltpu.VMEM((rows, BLOCK), jnp.float32),
        pltpu.VMEM((GROUP, rows, HEAD_WIDTH), jnp.float32),
        pltpu.VMEM((GROUP, rows, 2 * HEAD_WIDTH), jnp.float32),
        pltpu.SemaphoreType.DMA((KV_SLOTS + 4,)),
    ]


def flash_cost(rows, more_flops, more_bytes):
    typical = 6
    return pl.CostEstimate(
        flops=typical * GROUP * rows * BLOCK * HEAD_WIDTH * 8 + more_flops,
        bytes_accessed=KV_SLOTS * BLOCK * HEAD_WIDTH * 4 + more_bytes,
        transcendentals=typical * GROUP * rows * BLOCK,
    )


def first_kernel(scalars, queries, low, *refs):
    blocks = refs[:KV_SLOTS]
    out, token, pairs, query, bias, highest, numer, done = refs[-8:]
    token[...] = jnp.zeros(token.shape, jnp.float32)
    copies = fetch(
        [queries.at[0], *blocks], [query] + [pairs.at[n] for n in range(KV_SLOTS)], done
    )
    rows = query.shape[0]
    high = scalars[0] * BLOCK + lax.broadcasted_iota(jnp.int32, (rows, 1), 0)
    span_of = span(scalars, low[...].astype(jnp.float32))
    for copy in copies:
        copy.wait()
    flash(span_of, query, low[...], high, pairs, bias, highest, numer)
    store_heads(numer, out)


def attend_first(scalars, queries, low, blocks):
    _, rows, width = queries.shape
    return pl.pallas_call(
        first_kernel,
        out_shape=[jax.ShapeDtypeStruct((rows, width), jnp.bfloat16), TOKEN],
        in_specs=[SMEM, ANY, VMEM] + [ANY] * KV_SLOTS,
        out_specs=[VMEM, VMEM],
        scratch_shapes=flash_scratch(rows, rows, width),
        compiler_params=pltpu.CompilerParams(vmem_limit_bytes=58 * MIB),
        cost_estimate=flash_cost(rows, 0, 4 * rows * width),
    )(scalars, queries, low, *blocks)


def prepare_kernel(scalars, queries, routes, docs, residual, *refs):
    picked, table, low_out, slot_low, slot_high, slot_resid = refs[:6]
    query, features_in, routes_in, docs_in, done = refs[6:]
    copies = fetch(
        [routes, docs, queries.at[1], residual], [routes_in, docs_in, query, features_in], done
    )
    rows, tokens = table.shape
    copies[0].wait()
    copies[1].wait()
    across = tokens // docs_in.shape[1]
    own_docs = jnp.concatenate(
        [docs_in[pl.ds(scalars[0] * across + k, 1), :] for k in range(across)], axis=1
    )
    low = jnp.zeros((1, tokens), jnp.float32)
    for number in range(1, DOCS):
        before = jnp.where(docs_in[...] < number, 1.0, 0.0)
        before = jnp.sum(jnp.sum(before, axis=0, keepdims=True), axis=1, keepdims=True)
        low = jnp.where(own_docs == number, before, low)
    low_out[...] = low.astype(jnp.int32)
    route = routes_in[...]
    earlier = lax.broadcasted_iota(jnp.int32, (tokens, tokens), 0)
    earlier = earlier <= lax.broadcasted_iota(jnp.int32, (tokens, tokens), 1)
    named = lax.broadcasted_iota(jnp.int32, (16, tokens), 0) == route
    rank = jnp.dot(
        jnp.where(named, 1.0, 0.0).astype(jnp.bfloat16),
        jnp.where(earlier, 1.0, 0.0).astype(jnp.bfloat16),
        preferred_element_type=jnp.float32,
    )
    rank = rank.astype(jnp.int32) - 1
    number = lax.broadcasted_iota(jnp.int32, (PADDED_CAP, tokens), 0)
    for expert in range(rows // PADDED_CAP):
        placed = (rank[expert : expert + 1, :] == number) & (route == expert)
        table[expert * PADDED_CAP : (expert + 1) * PADDED_CAP, :] = jnp.where(
            placed, 1.0, 0.0
        ).astype(jnp.bfloat16)
    chosen = table[...]
    start = scalars[0] * BLOCK
    place = start + lax.broadcasted_iota(jnp.int32, (1, tokens), 1)
    held = chosen.astype(jnp.float32)
    first = jnp.sum(held * low, axis=1, keepdims=True)
    last = jnp.sum(held * place.astype(jnp.float32), axis=1, keepdims=True)
    slot_low[...] = first.astype(jnp.int32)
    slot_high[...] = jnp.maximum(last.astype(jnp.int32), start)
    for copy in copies[2:]:
        copy.wait()
    picked[...] = jnp.dot(chosen, query[...], preferred_element_type=jnp.float32).astype(
        jnp.bfloat16
    )
    slot_resid[...] = lax.dot_general(
        chosen, features_in[...], (((1,), (1,)), ((), ())), preferred_element_type=jnp.float32
    ).astype(jnp.bfloat16)


def prepare_slots(scalars, queries, routes, docs, residual, rows):
    _, tokens, width = queries.shape
    return pl.pallas_call(
        prepare_kernel,
        out_shape=[
            jax.ShapeDtypeStruct((rows, width), jnp.bfloat16),
            jax.ShapeDtypeStruct((rows, tokens), jnp.bfloat16),
            jax.ShapeDtypeStruct((1, tokens), jnp.int32),
            jax.ShapeDtypeStruct((rows, 1), jnp.int32),
            jax.ShapeDtypeStruct((rows, 1), jnp.int32),
            jax.ShapeDtypeStruct((rows, residual.shape[0]), jnp.bfloat16),
        ],
        in_specs=[SMEM, ANY, ANY, ANY, ANY],
        out_specs=[VMEM] * 6,
        scratch_shapes=[
            pltpu.VMEM((tokens, width), jnp.bfloat16),
            pltpu.VMEM(residual.shape, jnp.bfloat16),
            pltpu.VMEM(routes.shape, jnp.int32),
            pltpu.VMEM(docs.shape, jnp.int32),
            pltpu.SemaphoreType.DMA((4,)),
        ],
        compiler_params=pltpu.CompilerParams(vmem_limit_bytes=40 * MIB),
        cost_estimate=pl.CostEstimate(
            flops=2 * rows * tokens * 4 * width, bytes_accessed=8 * MIB, transcendentals=0
        ),
    )(scalars, queries, routes, docs, residual)


def slots_kernel(scalars, picked, low, slot_low, slot_high, slot_resid, weight, *refs):
    blocks = refs[:KV_SLOTS]
    out, pairs, bias, highest, numer, mix, product, done = refs[KV_SLOTS:]
    copies = fetch(blocks, [pairs.at[n] for n in range(KV_SLOTS)], done)
    span_of = span(scalars, low[...].astype(jnp.float32))
    for copy in copies:
        copy.wait()
    flash(span_of, picked, slot_low[...], slot_high[...], pairs, bias, highest, numer)
    store_heads(numer, mix)
    product[...] = jnp.dot(mix[...], weight[...], preferred_element_type=jnp.float32)
    features = slot_resid.shape[1]
    for part in range(product.shape[1] // features):

        @pl.when(scalars[1] == part)
        def _():
            product[:, part * features : (part + 1) * features] += slot_resid[...].astype(
                jnp.float32
            )

    width = product.shape[1]
    for part in range(out.shape[0]):
        base = part // 2 * PADDED_CAP + part % 2 * SHARE
        whole = SHARE // SUB
        for group in range(whole):
            at = base + group * SUB
            out[part, :, group * width : (group + 1) * width] = product[
                at : at + SUB, :
            ].astype(jnp.bfloat16)
        rest = product[base + whole * SUB : base + SHARE, :]
        rest = jnp.concatenate([rest[:, : width // 2], rest[:, width // 2 :]], axis=0)
        out[part, :, whole * width :] = rest.astype(jnp.bfloat16)


def attend_slots(scalars, picked, low, slot_low, slot_high, slot_resid, weight, blocks):
    rows, width = picked.shape
    out_width = weight.shape[1]
    scratch = flash_scratch(rows, rows, width)
    return pl.pallas_call(
        slots_kernel,
        out_shape=jax.ShapeDtypeStruct(
            (2 * rows // PADDED_CAP, SUB, SHARE * out_width // SUB), jnp.bfloat16
        ),
        in_specs=[SMEM] + [VMEM] * 6 + [ANY] * KV_SLOTS,
        out_specs=VMEM,
        scratch_shapes=[scratch[0], *scratch[2:5]]
        + [
            pltpu.VMEM((rows, width), jnp.bfloat16),
            pltpu.VMEM((rows, out_width), jnp.float32),
            scratch[5],
        ],
        compiler_params=pltpu.CompilerParams(vmem_limit_bytes=SLOTS_VMEM * MIB),
        cost_estimate=flash_cost(rows, 2 * rows * width * out_width, 2 * width * out_width),
    )(scalars, picked, low, slot_low, slot_high, slot_resid, weight, *blocks)


def norm_kernel(shares, gain, *refs):
    out = refs[-1]
    total = shares[0].astype(jnp.float32)
    for number in range(1, shares.shape[0]):
        total = total + shares[number].astype(jnp.float32)
    rows, width = out.shape
    whole = SHARE // SUB
    groups = [total[:, group * width : (group + 1) * width] for group in range(whole)]
    rest = total[:, whole * width :]
    groups.append(jnp.concatenate([rest[: SUB // 2], rest[SUB // 2 :]], axis=1))
    groups.append(jnp.zeros((rows - SHARE, width), jnp.float32))
    state = jnp.concatenate(groups, axis=0)
    mean_square = jnp.mean(state * state, axis=1, keepdims=True)
    out[...] = (state * lax.rsqrt(mean_square + norm_eps) * gain[...]).astype(jnp.bfloat16)


def normalize(shares, norm_gain, after):
    count = shares.shape[0]
    rows, width = HALF, norm_gain.shape[0]
    return pl.pallas_call(
        norm_kernel,
        out_shape=jax.ShapeDtypeStruct((rows, width), jnp.bfloat16),
        in_specs=[VMEM, VMEM] + [VMEM] * len(after),
        out_specs=VMEM,
        compiler_params=pltpu.CompilerParams(vmem_limit_bytes=24 * MIB),
        cost_estimate=pl.CostEstimate(
            flops=count * rows * width * 3,
            bytes_accessed=(count + 1) * rows * width * 2,
            transcendentals=rows,
        ),
    )(shares, norm_gain.reshape(1, width), *after)


def hidden_kernel(offsets, *refs):
    pieces = len(offsets)
    rows_in, weights_in = refs[:pieces], refs[pieces : pieces + 4]
    act, rows, weights, total = refs[pieces + 4 :]
    step = pl.program_id(0)
    units = weights_in[0].shape[0]

    @pl.when(step == 0)
    def _():
        rows[...] = jnp.zeros(rows.shape, jnp.bfloat16)
        total[...] = jnp.zeros(total.shape, jnp.float32)

    for offset, piece in zip(offsets, rows_in):
        rows[offset : offset + piece.shape[0], :] = piece[...]
    for number in range(4):
        weights[number * units : (number + 1) * units, :] = weights_in[number][...]
    total[...] += lax.dot_general(
        rows[...],
        weights[...],
        (((1,), (1,)), ((), ())),
        preferred_element_type=jnp.float32,
    )

    @pl.when(step == pl.num_programs(0) - 1)
    def _():
        gate = total[:, : 2 * units]
        up = total[:, 2 * units :]
        act[...] = (gate / (1.0 + jnp.exp(-gate)) * up).astype(jnp.bfloat16)


def hidden(row_pieces, weights):
    offsets, flat = [], []
    for number, parts in enumerate(row_pieces):
        offset = number * PADDED_CAP
        for part in parts:
            offsets.append(offset)
            flat.append(part)
            offset += part.shape[0]
    width = flat[0].shape[1]
    units = weights[0].shape[0]
    rows = len(row_pieces) * PADDED_CAP
    chunk = 1280
    weight_spec = pl.BlockSpec((units, chunk), lambda i: (0, i))
    return pl.pallas_call(
        functools.partial(hidden_kernel, tuple(offsets)),
        grid=(width // chunk,),
        out_shape=jax.ShapeDtypeStruct((rows, 2 * units), jnp.bfloat16),
        in_specs=[pl.BlockSpec((part.shape[0], chunk), lambda i: (0, i)) for part in flat]
        + [weight_spec] * 4,
        out_specs=pl.BlockSpec((rows, 2 * units), lambda i: (0, 0)),
        scratch_shapes=[
            pltpu.VMEM((rows, chunk), jnp.bfloat16),
            pltpu.VMEM((4 * units, chunk), jnp.bfloat16),
            pltpu.VMEM((rows, 4 * units), jnp.float32),
        ],
        compiler_params=pltpu.CompilerParams(vmem_limit_bytes=40 * MIB),
        cost_estimate=pl.CostEstimate(
            flops=8 * rows * width * units,
            bytes_accessed=2 * rows * width + 8 * width * units,
            transcendentals=2 * rows * units,
        ),
    )(*flat, *weights)


def down_kernel(places, act, down_own, down_other, out, weights, product):
    units = down_own.shape[0]
    pieces, parts = out.shape[:2]
    features = product.shape[1] // parts
    weights[:units, :] = down_own[...]
    weights[units:, :] = down_other[...]
    product[...] = jnp.dot(act[...], weights[...], preferred_element_type=jnp.float32)
    for number in range(pieces):
        place = places[number]
        for part in range(parts):
            for group in range(CAP // SUB):
                at = number * PADDED_CAP + group * SUB
                out[place, part, :, group * features : (group + 1) * features] = product[
                    at : at + SUB, part * features : (part + 1) * features
                ].astype(jnp.bfloat16)


def down(places, act, downs, parts):
    rows = act.shape[0]
    units, width = downs[0].shape
    pieces = rows // PADDED_CAP
    packed = (SUB, CAP // SUB * (width // parts))
    steps = 2
    weight_spec = pl.BlockSpec((units, width // steps), lambda i: (0, i))
    return pl.pallas_call(
        down_kernel,
        grid=(steps,),
        out_shape=jax.ShapeDtypeStruct((pieces, parts, *packed), jnp.bfloat16),
        in_specs=[SMEM, pl.BlockSpec(act.shape, lambda i: (0, 0)), weight_spec, weight_spec],
        out_specs=pl.BlockSpec((pieces, parts // steps, *packed), lambda i: (0, i, 0, 0)),
        scratch_shapes=[
            pltpu.VMEM((2 * units, width // steps), jnp.bfloat16),
            pltpu.VMEM((rows, width // steps), jnp.float32),
        ],
        compiler_params=pltpu.CompilerParams(vmem_limit_bytes=48 * MIB),
        cost_estimate=pl.CostEstimate(
            flops=4 * rows * width * units,
            bytes_accessed=2 * rows * width + 4 * width * units,
            transcendentals=0,
        ),
    )(places, act, *downs)


def collect_kernel(shares, table, out, merged):
    step = pl.program_id(0)
    sources, _, halves, sub, packed = shares.shape
    features = merged.shape[2]
    total = jnp.zeros((sub, packed), jnp.float32)
    for source in range(sources):
        for half in range(halves):
            total = total + shares[source, 0, half].astype(jnp.float32)
    groups = [total[:, at : at + features] for at in range(0, packed, features)]
    groups.append(jnp.zeros((PADDED_CAP - CAP, features), jnp.float32))
    merged[step] = jnp.concatenate(groups, axis=0).astype(jnp.bfloat16)

    @pl.when(step == pl.num_programs(0) - 1)
    def _():
        experts = merged.shape[0]
        stacked = merged[...].reshape(experts * PADDED_CAP, features)
        out[...] = lax.dot_general(
            stacked, table[...], (((0,), (0,)), ((), ())), preferred_element_type=jnp.float32
        ).astype(jnp.bfloat16)


def collect(shares, table):
    sources, experts, halves, sub, packed = shares.shape
    features = packed * sub // CAP
    tokens = table.shape[1]
    return pl.pallas_call(
        collect_kernel,
        grid=(experts,),
        out_shape=jax.ShapeDtypeStruct((features, tokens), jnp.bfloat16),
        in_specs=[
            pl.BlockSpec((sources, 1, halves, sub, packed), lambda i: (0, i, 0, 0, 0)),
            pl.BlockSpec(table.shape, lambda i: (0, 0)),
        ],
        out_specs=pl.BlockSpec((features, tokens), lambda i: (0, 0)),
        scratch_shapes=[pltpu.VMEM((experts, PADDED_CAP, features), jnp.bfloat16)],
        compiler_params=pltpu.CompilerParams(vmem_limit_bytes=24 * MIB),
        cost_estimate=pl.CostEstimate(
            flops=2 * tokens * table.shape[0] * features,
            bytes_accessed=2 * shares.size + 2 * tokens * features,
            transcendentals=0,
        ),
    )(shares, table)


def shards(
    queries,
    common_keys,
    common_values,
    doc_ids,
    routes,
    residual,
    out_weight,
    norm_gain,
    gate_weight,
    up_weight,
    down_weight,
):
    ctx_size = lax.axis_size("ctx")
    exp_size = lax.axis_size("exp")
    chips = ctx_size // 2
    in_flight = exp_size // 2
    tokens = queries.shape[1]
    features = residual.shape[1]
    ctx = lax.axis_index("ctx")
    exp = lax.axis_index("exp")
    chip, core = ctx // 2, ctx % 2
    swap_cores = [(c, c ^ 1) for c in range(ctx_size)]

    own = jnp.concatenate([common_keys, common_values], axis=1)
    mine = [own] + [
        lax.ppermute(own, "ctx", [(c, c + 2 * s) for c in range(ctx_size - 2 * s)])
        for s in range(1, BACK + 1)
    ]
    scalars = jnp.stack([ctx, exp]).astype(jnp.int32)
    picked, table, low, slot_low, slot_high, slot_resid = prepare_slots(
        scalars,
        queries,
        routes.reshape(1, tokens),
        doc_ids.reshape(-1, 128),
        residual.T,
        in_flight * PADDED_CAP,
    )
    theirs = [
        lax.ppermute(lax.optimization_barrier((block, slot_high))[0], "ctx", swap_cores)
        for block in mine
    ]
    blocks = mine + theirs
    product = attend_slots(
        scalars, picked, low, slot_low, slot_high, slot_resid, out_weight, blocks
    )
    shares = lax.all_to_all(product, "exp", 0, 0, tiled=True)
    low, _ = lax.optimization_barrier((low, product))
    first_attention, first_done = attend_first(scalars, queries, low.reshape(tokens, 1), blocks)
    gate, up, down_own = gate_weight[0].T, up_weight[0].T, down_weight[0]
    gate, up, down_own, _ = lax.optimization_barrier((gate, up, down_own, low))
    gate_other, up_other, down_other = (
        lax.ppermute(weight, "ctx", swap_cores) for weight in (gate, up, down_own)
    )
    swapped = gate_other[:8, :128] + up_other[:8, :128] + down_other[:8, :128]
    normed = normalize(shares, norm_gain, after=(first_done + swapped.astype(jnp.float32),))

    pair = [(e, e ^ 1) for e in range(exp_size)]
    other = lax.ppermute(normed, "exp", pair)
    odd = exp % 2 == 1
    block = jnp.concatenate(
        [jnp.where(odd, other, normed)[:SHARE], jnp.where(odd, normed, other)[:SHARE]], axis=0
    )
    ring = chips // 2

    def beside(c, distance):
        chip_of, core_of = c // 2, c % 2
        place = (chip_of % ring + distance) % ring
        return (chip_of // ring * ring + place) * 2 + core_of

    right = [(c, beside(c, 1)) for c in range(ctx_size)]
    left = [(c, beside(c, -1)) for c in range(ctx_size)]
    across = [(c, (c + ctx_size // 2) % ctx_size) for c in range(ctx_size)]
    from_left = lax.ppermute(block, "ctx", right)
    from_right = lax.ppermute(block, "ctx", left)
    far = lax.ppermute(block, "ctx", across)
    opposite_top = lax.ppermute(from_left[:SPLIT], "ctx", right)
    opposite_rest = lax.ppermute(from_right[SPLIT:], "ctx", left)
    far_next, _, _ = lax.optimization_barrier((far, from_left, from_right))
    far_left = lax.ppermute(far_next, "ctx", right)
    far_right = lax.ppermute(far_next, "ctx", left)
    far_opposite_top = lax.ppermute(opposite_top, "ctx", across)
    far_opposite_rest = lax.ppermute(opposite_rest, "ctx", across)
    pieces = [
        (block,),
        (far,),
        (from_left,),
        (from_right,),
        (far_left,),
        (far_right,),
        (opposite_top, opposite_rest),
        (far_opposite_top, far_opposite_rest),
    ]
    row, along = chip // ring, chip % ring
    places = jnp.stack(
        [
            (row ^ z) * ring + (along + x) % ring
            for z, x in (
                (0, 0), (1, 0), (0, ring - 1), (0, 1), (1, ring - 1), (1, 1), (0, 2), (1, 2)
            )
        ]
    ).astype(jnp.int32)

    act = hidden(pieces, (gate, gate_other, up, up_other))
    partial = down(places, act, (down_own, down_other), exp_size)
    same_core = [
        [c * exp_size + e for c in range(k, ctx_size, 2) for e in range(exp_size)]
        for k in range(2)
    ]
    returned = lax.all_to_all(
        partial.reshape(chips * exp_size, *partial.shape[2:]),
        ("ctx", "exp"),
        0,
        0,
        tiled=True,
        axis_index_groups=same_core,
    )
    expert_output = collect(returned.reshape(chips, in_flight, 2, *partial.shape[2:]), table)
    return (first_attention, expert_output.T)


def solution(mesh):
    in_specs = (
        P(None, "ctx", "exp"),
        P("ctx", "exp"),
        P("ctx", "exp"),
        P(),
        P("ctx", None),
        P("ctx", "exp"),
        P("exp", None),
        P(),
        P("exp", None, "ctx"),
        P("exp", None, "ctx"),
        P("exp", "ctx", None),
    )
    out_specs = (P("ctx", "exp"), P("ctx", "exp"))
    return jax.shard_map(shards, mesh=mesh, in_specs=in_specs, out_specs=out_specs, check_vma=False)
```

```python
import functools

import jax
import jax.numpy as jnp
from jax import lax
from jax.experimental import pallas as pl
from jax.experimental.pallas import tpu as pltpu
from jax.sharding import PartitionSpec as P

QUERY_HEAD_COUNT = 40
SHARED_KV_HEADS = 8
HEAD_WIDTH = 128
CAP = 40
DOCS = 6

GROUP = QUERY_HEAD_COUNT // SHARED_KV_HEADS
BLOCK = 512
BACK = 4
KV_SLOTS = 2 * (BACK + 1)
PADDED_CAP = 48
HALF = PADDED_CAP // 2
SHARE = CAP // 2
SUB = 8
MIB = 1 << 20
SLOTS_VMEM = 51
TILE = 256

big_negative = -1e30
norm_eps = 1e-06
log2e = 1.4426950408889634

VMEM = pl.BlockSpec(memory_space=pltpu.VMEM)
SMEM = pl.BlockSpec(memory_space=pltpu.SMEM)
ANY = pl.BlockSpec(memory_space=pl.ANY)
TOKEN = jax.ShapeDtypeStruct((8, 128), jnp.float32)


def fetch(sources, targets, done):
    copies = [
        pltpu.make_async_copy(source, target, done.at[number])
        for number, (source, target) in enumerate(zip(sources, targets))
    ]
    for copy in copies:
        copy.start()
    return copies


def span(scalars, low):
    chip, core = scalars[0] // 2, scalars[0] % 2
    base = 2 * (chip - BACK)
    first = jnp.min(low).astype(jnp.int32) // BLOCK - base
    return first, 2 * BACK + core, core, base


def flash(span_of, query, low, high, pairs, bias, highest, numer):
    first, last, core, base = span_of
    rows = query.shape[0]
    highest[...] = jnp.full(highest.shape, big_negative, jnp.float32)
    numer[...] = jnp.zeros(numer.shape, jnp.float32)
    scale = float(HEAD_WIDTH) ** (-0.5) * log2e
    ones = jnp.ones((BLOCK, HEAD_WIDTH), jnp.bfloat16)
    tile = TILE if rows % TILE == 0 else rows
    tops = range(0, rows, tile)

    def hide(at):
        place = (base + at) * BLOCK + lax.broadcasted_iota(jnp.int32, (rows, BLOCK), 1)
        seen = (place >= low) & (place <= high)
        bias[...] = jnp.where(seen, 0.0, big_negative)
        return BACK - at // 2 + jnp.where(at % 2 == core, 0, BACK + 1)

    def score(head, part, key_block):
        scores = lax.dot_general(
            query[part, head * HEAD_WIDTH : (head + 1) * HEAD_WIDTH],
            key_block,
            (((1,), (1,)), ((), ())),
            preferred_element_type=jnp.float32,
        )
        return scores + bias[part, :]

    def find_highest(at, carry):
        key_block = pairs[hide(at), :, :HEAD_WIDTH]
        for head in range(GROUP):
            for top in tops:
                part = slice(top, top + tile)
                scores = score(head, part, key_block)
                most = highest[head, part]
                for lane in range(0, BLOCK, HEAD_WIDTH):
                    most = jnp.maximum(most, scores[:, lane : lane + HEAD_WIDTH])
                highest[head, part] = most
        return carry

    lax.fori_loop(first, last + 1, find_highest, 0)
    for head in range(GROUP):
        most = jnp.max(highest[head], axis=1, keepdims=True)
        highest[head] = jnp.broadcast_to(most, (rows, HEAD_WIDTH))

    def add_block(at, carry):
        slot = hide(at)
        key_block = pairs[slot, :, :HEAD_WIDTH]
        value_block = jnp.concatenate([pairs[slot, :, HEAD_WIDTH:], ones], axis=1)
        for head in range(GROUP):
            for top in tops:
                part = slice(top, top + tile)
                most = jnp.concatenate([highest[head, part]] * (BLOCK // HEAD_WIDTH), axis=1)
                probs = jnp.exp2((score(head, part, key_block) - most) * scale)
                numer[head, part] += jnp.dot(
                    probs.astype(jnp.bfloat16), value_block, preferred_element_type=jnp.float32
                )
        return carry

    lax.fori_loop(first, last + 1, add_block, 0)


def store_heads(numer, out):
    for head in range(GROUP):
        summed = numer[head]
        out[:, head * HEAD_WIDTH : (head + 1) * HEAD_WIDTH] = (
            summed[:, :HEAD_WIDTH] / summed[:, HEAD_WIDTH:]
        ).astype(jnp.bfloat16)


def flash_scratch(rows, tokens, width):
    return [
        pltpu.VMEM((KV_SLOTS, BLOCK, 2 * HEAD_WIDTH), jnp.bfloat16),
        pltpu.VMEM((tokens, width), jnp.bfloat16),
        pltpu.VMEM((rows, BLOCK), jnp.float32),
        pltpu.VMEM((GROUP, rows, HEAD_WIDTH), jnp.float32),
        pltpu.VMEM((GROUP, rows, 2 * HEAD_WIDTH), jnp.float32),
        pltpu.SemaphoreType.DMA((KV_SLOTS + 4,)),
    ]


def flash_cost(rows, more_flops, more_bytes):
    typical = 6
    return pl.CostEstimate(
        flops=typical * GROUP * rows * BLOCK * HEAD_WIDTH * 8 + more_flops,
        bytes_accessed=KV_SLOTS * BLOCK * HEAD_WIDTH * 4 + more_bytes,
        transcendentals=typical * GROUP * rows * BLOCK,
    )


def first_kernel(scalars, queries, low, *refs):
    blocks = refs[:KV_SLOTS]
    out, token, pairs, query, bias, highest, numer, done = refs[-8:]
    token[...] = jnp.zeros(token.shape, jnp.float32)
    copies = fetch(
        [queries.at[0], *blocks], [query] + [pairs.at[n] for n in range(KV_SLOTS)], done
    )
    rows = query.shape[0]
    high = scalars[0] * BLOCK + lax.broadcasted_iota(jnp.int32, (rows, 1), 0)
    span_of = span(scalars, low[...].astype(jnp.float32))
    for copy in copies:
        copy.wait()
    flash(span_of, query, low[...], high, pairs, bias, highest, numer)
    store_heads(numer, out)


def attend_first(scalars, queries, low, blocks):
    _, rows, width = queries.shape
    return pl.pallas_call(
        first_kernel,
        out_shape=[jax.ShapeDtypeStruct((rows, width), jnp.bfloat16), TOKEN],
        in_specs=[SMEM, ANY, VMEM] + [ANY] * KV_SLOTS,
        out_specs=[VMEM, VMEM],
        scratch_shapes=flash_scratch(rows, rows, width),
        compiler_params=pltpu.CompilerParams(vmem_limit_bytes=58 * MIB),
        cost_estimate=flash_cost(rows, 0, 4 * rows * width),
    )(scalars, queries, low, *blocks)


def prepare_kernel(scalars, queries, routes, docs, residual, *refs):
    picked, table, low_out, slot_low, slot_high, slot_resid = refs[:6]
    query, features_in, routes_in, docs_in, done = refs[6:]
    copies = fetch(
        [routes, docs, queries.at[1], residual], [routes_in, docs_in, query, features_in], done
    )
    rows, tokens = table.shape
    copies[0].wait()
    copies[1].wait()
    across = tokens // docs_in.shape[1]
    own_docs = jnp.concatenate(
        [docs_in[pl.ds(scalars[0] * across + k, 1), :] for k in range(across)], axis=1
    )
    low = jnp.zeros((1, tokens), jnp.float32)
    for number in range(1, DOCS):
        before = jnp.where(docs_in[...] < number, 1.0, 0.0)
        before = jnp.sum(jnp.sum(before, axis=0, keepdims=True), axis=1, keepdims=True)
        low = jnp.where(own_docs == number, before, low)
    low_out[...] = low.astype(jnp.int32)
    route = routes_in[...]
    earlier = lax.broadcasted_iota(jnp.int32, (tokens, tokens), 0)
    earlier = earlier <= lax.broadcasted_iota(jnp.int32, (tokens, tokens), 1)
    named = lax.broadcasted_iota(jnp.int32, (16, tokens), 0) == route
    rank = jnp.dot(
        jnp.where(named, 1.0, 0.0).astype(jnp.bfloat16),
        jnp.where(earlier, 1.0, 0.0).astype(jnp.bfloat16),
        preferred_element_type=jnp.float32,
    )
    rank = rank.astype(jnp.int32) - 1
    number = lax.broadcasted_iota(jnp.int32, (PADDED_CAP, tokens), 0)
    for expert in range(rows // PADDED_CAP):
        placed = (rank[expert : expert + 1, :] == number) & (route == expert)
        table[expert * PADDED_CAP : (expert + 1) * PADDED_CAP, :] = jnp.where(
            placed, 1.0, 0.0
        ).astype(jnp.bfloat16)
    chosen = table[...]
    start = scalars[0] * BLOCK
    place = start + lax.broadcasted_iota(jnp.int32, (1, tokens), 1)
    held = chosen.astype(jnp.float32)
    first = jnp.sum(held * low, axis=1, keepdims=True)
    last = jnp.sum(held * place.astype(jnp.float32), axis=1, keepdims=True)
    slot_low[...] = first.astype(jnp.int32)
    slot_high[...] = jnp.maximum(last.astype(jnp.int32), start)
    for copy in copies[2:]:
        copy.wait()
    picked[...] = jnp.dot(chosen, query[...], preferred_element_type=jnp.float32).astype(
        jnp.bfloat16
    )
    slot_resid[...] = lax.dot_general(
        chosen, features_in[...], (((1,), (1,)), ((), ())), preferred_element_type=jnp.float32
    ).astype(jnp.bfloat16)


def prepare_slots(scalars, queries, routes, docs, residual, rows):
    _, tokens, width = queries.shape
    return pl.pallas_call(
        prepare_kernel,
        out_shape=[
            jax.ShapeDtypeStruct((rows, width), jnp.bfloat16),
            jax.ShapeDtypeStruct((rows, tokens), jnp.bfloat16),
            jax.ShapeDtypeStruct((1, tokens), jnp.int32),
            jax.ShapeDtypeStruct((rows, 1), jnp.int32),
            jax.ShapeDtypeStruct((rows, 1), jnp.int32),
            jax.ShapeDtypeStruct((rows, residual.shape[0]), jnp.bfloat16),
        ],
        in_specs=[SMEM, ANY, ANY, ANY, ANY],
        out_specs=[VMEM] * 6,
        scratch_shapes=[
            pltpu.VMEM((tokens, width), jnp.bfloat16),
            pltpu.VMEM(residual.shape, jnp.bfloat16),
            pltpu.VMEM(routes.shape, jnp.int32),
            pltpu.VMEM(docs.shape, jnp.int32),
            pltpu.SemaphoreType.DMA((4,)),
        ],
        compiler_params=pltpu.CompilerParams(vmem_limit_bytes=40 * MIB),
        cost_estimate=pl.CostEstimate(
            flops=2 * rows * tokens * 4 * width, bytes_accessed=8 * MIB, transcendentals=0
        ),
    )(scalars, queries, routes, docs, residual)


def slots_kernel(scalars, picked, low, slot_low, slot_high, slot_resid, weight, *refs):
    blocks = refs[:KV_SLOTS]
    out, pairs, bias, highest, numer, mix, product, done = refs[KV_SLOTS:]
    copies = fetch(blocks, [pairs.at[n] for n in range(KV_SLOTS)], done)
    span_of = span(scalars, low[...].astype(jnp.float32))
    for copy in copies:
        copy.wait()
    flash(span_of, picked, slot_low[...], slot_high[...], pairs, bias, highest, numer)
    store_heads(numer, mix)
    product[...] = jnp.dot(mix[...], weight[...], preferred_element_type=jnp.float32)
    features = slot_resid.shape[1]
    for part in range(product.shape[1] // features):

        @pl.when(scalars[1] == part)
        def _():
            product[:, part * features : (part + 1) * features] += slot_resid[...].astype(
                jnp.float32
            )

    width = product.shape[1]
    for part in range(out.shape[0]):
        base = part // 2 * PADDED_CAP + part % 2 * SHARE
        whole = SHARE // SUB
        for group in range(whole):
            at = base + group * SUB
            out[part, :, group * width : (group + 1) * width] = product[
                at : at + SUB, :
            ].astype(jnp.bfloat16)
        rest = product[base + whole * SUB : base + SHARE, :]
        rest = jnp.concatenate([rest[:, : width // 2], rest[:, width // 2 :]], axis=0)
        out[part, :, whole * width :] = rest.astype(jnp.bfloat16)


def attend_slots(scalars, picked, low, slot_low, slot_high, slot_resid, weight, blocks):
    rows, width = picked.shape
    out_width = weight.shape[1]
    scratch = flash_scratch(rows, rows, width)
    return pl.pallas_call(
        slots_kernel,
        out_shape=jax.ShapeDtypeStruct(
            (2 * rows // PADDED_CAP, SUB, SHARE * out_width // SUB), jnp.bfloat16
        ),
        in_specs=[SMEM] + [VMEM] * 6 + [ANY] * KV_SLOTS,
        out_specs=VMEM,
        scratch_shapes=[scratch[0], *scratch[2:5]]
        + [
            pltpu.VMEM((rows, width), jnp.bfloat16),
            pltpu.VMEM((rows, out_width), jnp.float32),
            scratch[5],
        ],
        compiler_params=pltpu.CompilerParams(vmem_limit_bytes=SLOTS_VMEM * MIB),
        cost_estimate=flash_cost(rows, 2 * rows * width * out_width, 2 * width * out_width),
    )(scalars, picked, low, slot_low, slot_high, slot_resid, weight, *blocks)


def norm_kernel(shares, gain, *refs):
    out = refs[-1]
    total = shares[0].astype(jnp.float32)
    for number in range(1, shares.shape[0]):
        total = total + shares[number].astype(jnp.float32)
    rows, width = out.shape
    whole = SHARE // SUB
    groups = [total[:, group * width : (group + 1) * width] for group in range(whole)]
    rest = total[:, whole * width :]
    groups.append(jnp.concatenate([rest[: SUB // 2], rest[SUB // 2 :]], axis=1))
    groups.append(jnp.zeros((rows - SHARE, width), jnp.float32))
    state = jnp.concatenate(groups, axis=0)
    mean_square = jnp.mean(state * state, axis=1, keepdims=True)
    out[...] = (state * lax.rsqrt(mean_square + norm_eps) * gain[...]).astype(jnp.bfloat16)


def normalize(shares, norm_gain, after):
    count = shares.shape[0]
    rows, width = HALF, norm_gain.shape[0]
    return pl.pallas_call(
        norm_kernel,
        out_shape=jax.ShapeDtypeStruct((rows, width), jnp.bfloat16),
        in_specs=[VMEM, VMEM] + [VMEM] * len(after),
        out_specs=VMEM,
        compiler_params=pltpu.CompilerParams(vmem_limit_bytes=24 * MIB),
        cost_estimate=pl.CostEstimate(
            flops=count * rows * width * 3,
            bytes_accessed=(count + 1) * rows * width * 2,
            transcendentals=rows,
        ),
    )(shares, norm_gain.reshape(1, width), *after)


def hidden_kernel(offsets, *refs):
    pieces = len(offsets)
    rows_in, weights_in = refs[:pieces], refs[pieces : pieces + 4]
    act, rows, weights, total = refs[pieces + 4 :]
    step = pl.program_id(0)
    units = weights_in[0].shape[0]

    @pl.when(step == 0)
    def _():
        rows[...] = jnp.zeros(rows.shape, jnp.bfloat16)
        total[...] = jnp.zeros(total.shape, jnp.float32)

    for offset, piece in zip(offsets, rows_in):
        rows[offset : offset + piece.shape[0], :] = piece[...]
    for number in range(4):
        weights[number * units : (number + 1) * units, :] = weights_in[number][...]
    total[...] += lax.dot_general(
        rows[...],
        weights[...],
        (((1,), (1,)), ((), ())),
        preferred_element_type=jnp.float32,
    )

    @pl.when(step == pl.num_programs(0) - 1)
    def _():
        gate = total[:, : 2 * units]
        up = total[:, 2 * units :]
        act[...] = (gate / (1.0 + jnp.exp(-gate)) * up).astype(jnp.bfloat16)


def hidden(row_pieces, weights):
    offsets, flat = [], []
    for number, parts in enumerate(row_pieces):
        offset = number * PADDED_CAP
        for part in parts:
            offsets.append(offset)
            flat.append(part)
            offset += part.shape[0]
    width = flat[0].shape[1]
    units = weights[0].shape[0]
    rows = len(row_pieces) * PADDED_CAP
    chunk = 1280
    weight_spec = pl.BlockSpec((units, chunk), lambda i: (0, i))
    return pl.pallas_call(
        functools.partial(hidden_kernel, tuple(offsets)),
        grid=(width // chunk,),
        out_shape=jax.ShapeDtypeStruct((rows, 2 * units), jnp.bfloat16),
        in_specs=[pl.BlockSpec((part.shape[0], chunk), lambda i: (0, i)) for part in flat]
        + [weight_spec] * 4,
        out_specs=pl.BlockSpec((rows, 2 * units), lambda i: (0, 0)),
        scratch_shapes=[
            pltpu.VMEM((rows, chunk), jnp.bfloat16),
            pltpu.VMEM((4 * units, chunk), jnp.bfloat16),
            pltpu.VMEM((rows, 4 * units), jnp.float32),
        ],
        compiler_params=pltpu.CompilerParams(vmem_limit_bytes=40 * MIB),
        cost_estimate=pl.CostEstimate(
            flops=8 * rows * width * units,
            bytes_accessed=2 * rows * width + 8 * width * units,
            transcendentals=2 * rows * units,
        ),
    )(*flat, *weights)


def down_kernel(places, act, down_own, down_other, out, weights, product):
    units = down_own.shape[0]
    pieces, parts = out.shape[:2]
    features = product.shape[1] // parts
    weights[:units, :] = down_own[...]
    weights[units:, :] = down_other[...]
    product[...] = jnp.dot(act[...], weights[...], preferred_element_type=jnp.float32)
    for number in range(pieces):
        place = places[number]
        for part in range(parts):
            for group in range(CAP // SUB):
                at = number * PADDED_CAP + group * SUB
                out[place, part, :, group * features : (group + 1) * features] = product[
                    at : at + SUB, part * features : (part + 1) * features
                ].astype(jnp.bfloat16)


def down(places, act, downs, parts):
    rows = act.shape[0]
    units, width = downs[0].shape
    pieces = rows // PADDED_CAP
    packed = (SUB, CAP // SUB * (width // parts))
    steps = 2
    weight_spec = pl.BlockSpec((units, width // steps), lambda i: (0, i))
    return pl.pallas_call(
        down_kernel,
        grid=(steps,),
        out_shape=jax.ShapeDtypeStruct((pieces, parts, *packed), jnp.bfloat16),
        in_specs=[SMEM, pl.BlockSpec(act.shape, lambda i: (0, 0)), weight_spec, weight_spec],
        out_specs=pl.BlockSpec((pieces, parts // steps, *packed), lambda i: (0, i, 0, 0)),
        scratch_shapes=[
            pltpu.VMEM((2 * units, width // steps), jnp.bfloat16),
            pltpu.VMEM((rows, width // steps), jnp.float32),
        ],
        compiler_params=pltpu.CompilerParams(vmem_limit_bytes=48 * MIB),
        cost_estimate=pl.CostEstimate(
            flops=4 * rows * width * units,
            bytes_accessed=2 * rows * width + 4 * width * units,
            transcendentals=0,
        ),
    )(places, act, *downs)


def collect_kernel(shares, table, out, merged):
    step = pl.program_id(0)
    sources, _, halves, sub, packed = shares.shape
    features = merged.shape[2]
    total = jnp.zeros((sub, packed), jnp.float32)
    for source in range(sources):
        for half in range(halves):
            total = total + shares[source, 0, half].astype(jnp.float32)
    groups = [total[:, at : at + features] for at in range(0, packed, features)]
    groups.append(jnp.zeros((PADDED_CAP - CAP, features), jnp.float32))
    merged[step] = jnp.concatenate(groups, axis=0).astype(jnp.bfloat16)

    @pl.when(step == pl.num_programs(0) - 1)
    def _():
        experts = merged.shape[0]
        stacked = merged[...].reshape(experts * PADDED_CAP, features)
        out[...] = lax.dot_general(
            stacked, table[...], (((0,), (0,)), ((), ())), preferred_element_type=jnp.float32
        ).astype(jnp.bfloat16)


def collect(shares, table):
    sources, experts, halves, sub, packed = shares.shape
    features = packed * sub // CAP
    tokens = table.shape[1]
    return pl.pallas_call(
        collect_kernel,
        grid=(experts,),
        out_shape=jax.ShapeDtypeStruct((features, tokens), jnp.bfloat16),
        in_specs=[
            pl.BlockSpec((sources, 1, halves, sub, packed), lambda i: (0, i, 0, 0, 0)),
            pl.BlockSpec(table.shape, lambda i: (0, 0)),
        ],
        out_specs=pl.BlockSpec((features, tokens), lambda i: (0, 0)),
        scratch_shapes=[pltpu.VMEM((experts, PADDED_CAP, features), jnp.bfloat16)],
        compiler_params=pltpu.CompilerParams(vmem_limit_bytes=24 * MIB),
        cost_estimate=pl.CostEstimate(
            flops=2 * tokens * table.shape[0] * features,
            bytes_accessed=2 * shares.size + 2 * tokens * features,
            transcendentals=0,
        ),
    )(shares, table)


def shards(
    queries,
    common_keys,
    common_values,
    doc_ids,
    routes,
    residual,
    out_weight,
    norm_gain,
    gate_weight,
    up_weight,
    down_weight,
):
    ctx_size = lax.axis_size("ctx")
    exp_size = lax.axis_size("exp")
    chips = ctx_size // 2
    in_flight = exp_size // 2
    tokens = queries.shape[1]
    features = residual.shape[1]
    ctx = lax.axis_index("ctx")
    exp = lax.axis_index("exp")
    chip, core = ctx // 2, ctx % 2
    swap_cores = [(c, c ^ 1) for c in range(ctx_size)]

    own = jnp.concatenate([common_keys, common_values], axis=1)
    mine = [own] + [
        lax.ppermute(own, "ctx", [(c, c + 2 * s) for c in range(ctx_size - 2 * s)])
        for s in range(1, BACK + 1)
    ]
    scalars = jnp.stack([ctx, exp]).astype(jnp.int32)
    picked, table, low, slot_low, slot_high, slot_resid = prepare_slots(
        scalars,
        queries,
        routes.reshape(1, tokens),
        doc_ids.reshape(-1, 128),
        residual.T,
        in_flight * PADDED_CAP,
    )
    theirs = [
        lax.ppermute(lax.optimization_barrier((block, slot_high))[0], "ctx", swap_cores)
        for block in mine
    ]
    blocks = mine + theirs
    product = attend_slots(
        scalars, picked, low, slot_low, slot_high, slot_resid, out_weight, blocks
    )
    shares = lax.all_to_all(product, "exp", 0, 0, tiled=True)
    low, _ = lax.optimization_barrier((low, product))
    first_attention, first_done = attend_first(scalars, queries, low.reshape(tokens, 1), blocks)
    gate, up, down_own = gate_weight[0].T, up_weight[0].T, down_weight[0]
    gate, up, down_own, _ = lax.optimization_barrier((gate, up, down_own, low))
    gate_other, up_other, down_other = (
        lax.ppermute(weight, "ctx", swap_cores) for weight in (gate, up, down_own)
    )
    swapped = gate_other[:8, :128] + up_other[:8, :128] + down_other[:8, :128]
    normed = normalize(shares, norm_gain, after=(first_done + swapped.astype(jnp.float32),))

    pair = [(e, e ^ 1) for e in range(exp_size)]
    other = lax.ppermute(normed, "exp", pair)
    odd = exp % 2 == 1
    block = jnp.concatenate(
        [jnp.where(odd, other, normed)[:SHARE], jnp.where(odd, normed, other)[:SHARE]], axis=0
    )
    ring = chips // 2

    def beside(c, distance):
        chip_of, core_of = c // 2, c % 2
        place = (chip_of % ring + distance) % ring
        return (chip_of // ring * ring + place) * 2 + core_of

    right = [(c, beside(c, 1)) for c in range(ctx_size)]
    left = [(c, beside(c, -1)) for c in range(ctx_size)]
    across = [(c, (c + ctx_size // 2) % ctx_size) for c in range(ctx_size)]
    from_left = lax.ppermute(block, "ctx", right)
    from_right = lax.ppermute(block, "ctx", left)
    far = lax.ppermute(block, "ctx", across)
    opposite = lax.ppermute(block, "ctx", [(c, beside(c, 2)) for c in range(ctx_size)])
    far_left = lax.ppermute(far, "ctx", right)
    far_right = lax.ppermute(far, "ctx", left)
    far_opposite = lax.ppermute(opposite, "ctx", across)
    pieces = [
        (block,),
        (far,),
        (from_left,),
        (from_right,),
        (far_left,),
        (far_right,),
        (opposite,),
        (far_opposite,),
    ]
    row, along = chip // ring, chip % ring
    places = jnp.stack(
        [
            (row ^ z) * ring + (along + x) % ring
            for z, x in (
                (0, 0), (1, 0), (0, ring - 1), (0, 1), (1, ring - 1), (1, 1), (0, 2), (1, 2)
            )
        ]
    ).astype(jnp.int32)

    act = hidden(pieces, (gate, gate_other, up, up_other))
    partial = down(places, act, (down_own, down_other), exp_size)
    same_core = [
        [c * exp_size + e for c in range(k, ctx_size, 2) for e in range(exp_size)]
        for k in range(2)
    ]
    returned = lax.all_to_all(
        partial.reshape(chips * exp_size, *partial.shape[2:]),
        ("ctx", "exp"),
        0,
        0,
        tiled=True,
        axis_index_groups=same_core,
    )
    expert_output = collect(returned.reshape(chips, in_flight, 2, *partial.shape[2:]), table)
    return (first_attention, expert_output.T)


def solution(mesh):
    in_specs = (
        P(None, "ctx", "exp"),
        P("ctx", "exp"),
        P("ctx", "exp"),
        P(),
        P("ctx", None),
        P("ctx", "exp"),
        P("exp", None),
        P(),
        P("exp", None, "ctx"),
        P("exp", None, "ctx"),
        P("exp", "ctx", None),
    )
    out_specs = (P("ctx", "exp"), P("ctx", "exp"))
    return jax.shard_map(shards, mesh=mesh, in_specs=in_specs, out_specs=out_specs, check_vma=False)
```

```python
import functools

import jax
import jax.numpy as jnp
from jax import lax
from jax.experimental import pallas as pl
from jax.experimental.pallas import tpu as pltpu
from jax.sharding import PartitionSpec as P

QUERY_HEAD_COUNT = 40
SHARED_KV_HEADS = 8
HEAD_WIDTH = 128
CAP = 40
DOCS = 6

GROUP = QUERY_HEAD_COUNT // SHARED_KV_HEADS
BLOCK = 512
BACK = 4
KV_SLOTS = 2 * (BACK + 1)
PADDED_CAP = 48
HALF = PADDED_CAP // 2
SHARE = CAP // 2
SUB = 8
SPLIT = 16
MIB = 1 << 20
SLOTS_VMEM = 51
TILE = 256

big_negative = -1e30
norm_eps = 1e-06
log2e = 1.4426950408889634

VMEM = pl.BlockSpec(memory_space=pltpu.VMEM)
SMEM = pl.BlockSpec(memory_space=pltpu.SMEM)
ANY = pl.BlockSpec(memory_space=pl.ANY)
TOKEN = jax.ShapeDtypeStruct((8, 128), jnp.float32)


def fetch(sources, targets, done):
    copies = [
        pltpu.make_async_copy(source, target, done.at[number])
        for number, (source, target) in enumerate(zip(sources, targets))
    ]
    for copy in copies:
        copy.start()
    return copies


def span(scalars, low):
    chip, core = scalars[0] // 2, scalars[0] % 2
    base = 2 * (chip - BACK)
    first = jnp.min(low).astype(jnp.int32) // BLOCK - base
    return first, 2 * BACK + core, core, base


def flash(span_of, query, low, high, pairs, bias, highest, numer):
    first, last, core, base = span_of
    rows = query.shape[0]
    highest[...] = jnp.full(highest.shape, big_negative, jnp.float32)
    numer[...] = jnp.zeros(numer.shape, jnp.float32)
    scale = float(HEAD_WIDTH) ** (-0.5) * log2e
    ones = jnp.ones((BLOCK, HEAD_WIDTH), jnp.bfloat16)
    tile = TILE if rows % TILE == 0 else rows
    tops = range(0, rows, tile)

    def hide(at):
        place = (base + at) * BLOCK + lax.broadcasted_iota(jnp.int32, (rows, BLOCK), 1)
        seen = (place >= low) & (place <= high)
        bias[...] = jnp.where(seen, 0.0, big_negative)
        return BACK - at // 2 + jnp.where(at % 2 == core, 0, BACK + 1)

    def score(head, part, key_block):
        scores = lax.dot_general(
            query[part, head * HEAD_WIDTH : (head + 1) * HEAD_WIDTH],
            key_block,
            (((1,), (1,)), ((), ())),
            preferred_element_type=jnp.float32,
        )
        return scores + bias[part, :]

    def find_highest(at, carry):
        key_block = pairs[hide(at), :, :HEAD_WIDTH]
        for head in range(GROUP):
            for top in tops:
                part = slice(top, top + tile)
                scores = score(head, part, key_block)
                most = highest[head, part]
                for lane in range(0, BLOCK, HEAD_WIDTH):
                    most = jnp.maximum(most, scores[:, lane : lane + HEAD_WIDTH])
                highest[head, part] = most
        return carry

    lax.fori_loop(first, last + 1, find_highest, 0)
    for head in range(GROUP):
        most = jnp.max(highest[head], axis=1, keepdims=True)
        highest[head] = jnp.broadcast_to(most, (rows, HEAD_WIDTH))

    def add_block(at, carry):
        slot = hide(at)
        key_block = pairs[slot, :, :HEAD_WIDTH]
        value_block = jnp.concatenate([pairs[slot, :, HEAD_WIDTH:], ones], axis=1)
        for head in range(GROUP):
            for top in tops:
                part = slice(top, top + tile)
                most = jnp.concatenate([highest[head, part]] * (BLOCK // HEAD_WIDTH), axis=1)
                probs = jnp.exp2((score(head, part, key_block) - most) * scale)
                numer[head, part] += jnp.dot(
                    probs.astype(jnp.bfloat16), value_block, preferred_element_type=jnp.float32
                )
        return carry

    lax.fori_loop(first, last + 1, add_block, 0)


def store_heads(numer, out):
    for head in range(GROUP):
        summed = numer[head]
        out[:, head * HEAD_WIDTH : (head + 1) * HEAD_WIDTH] = (
            summed[:, :HEAD_WIDTH] / summed[:, HEAD_WIDTH:]
        ).astype(jnp.bfloat16)


def flash_scratch(rows, tokens, width):
    return [
        pltpu.VMEM((KV_SLOTS, BLOCK, 2 * HEAD_WIDTH), jnp.bfloat16),
        pltpu.VMEM((tokens, width), jnp.bfloat16),
        pltpu.VMEM((rows, BLOCK), jnp.float32),
        pltpu.VMEM((GROUP, rows, HEAD_WIDTH), jnp.float32),
        pltpu.VMEM((GROUP, rows, 2 * HEAD_WIDTH), jnp.float32),
        pltpu.SemaphoreType.DMA((KV_SLOTS + 4,)),
    ]


def flash_cost(rows, more_flops, more_bytes):
    typical = 6
    return pl.CostEstimate(
        flops=typical * GROUP * rows * BLOCK * HEAD_WIDTH * 8 + more_flops,
        bytes_accessed=KV_SLOTS * BLOCK * HEAD_WIDTH * 4 + more_bytes,
        transcendentals=typical * GROUP * rows * BLOCK,
    )


def first_kernel(scalars, queries, low, *refs):
    blocks = refs[:KV_SLOTS]
    out, token, pairs, query, bias, highest, numer, done = refs[-8:]
    token[...] = jnp.zeros(token.shape, jnp.float32)
    copies = fetch(
        [queries.at[0], *blocks], [query] + [pairs.at[n] for n in range(KV_SLOTS)], done
    )
    rows = query.shape[0]
    high = scalars[0] * BLOCK + lax.broadcasted_iota(jnp.int32, (rows, 1), 0)
    span_of = span(scalars, low[...].astype(jnp.float32))
    for copy in copies:
        copy.wait()
    flash(span_of, query, low[...], high, pairs, bias, highest, numer)
    store_heads(numer, out)


def attend_first(scalars, queries, low, blocks):
    _, rows, width = queries.shape
    return pl.pallas_call(
        first_kernel,
        out_shape=[jax.ShapeDtypeStruct((rows, width), jnp.bfloat16), TOKEN],
        in_specs=[SMEM, ANY, VMEM] + [ANY] * KV_SLOTS,
        out_specs=[VMEM, VMEM],
        scratch_shapes=flash_scratch(rows, rows, width),
        compiler_params=pltpu.CompilerParams(vmem_limit_bytes=58 * MIB),
        cost_estimate=flash_cost(rows, 0, 4 * rows * width),
    )(scalars, queries, low, *blocks)


def prepare_kernel(scalars, queries, routes, docs, residual, *refs):
    picked, table, low_out, slot_low, slot_high, slot_resid = refs[:6]
    query, features_in, routes_in, docs_in, done = refs[6:]
    copies = fetch(
        [routes, docs, queries.at[1], residual], [routes_in, docs_in, query, features_in], done
    )
    rows, tokens = table.shape
    copies[0].wait()
    copies[1].wait()
    across = tokens // docs_in.shape[1]
    own_docs = jnp.concatenate(
        [docs_in[pl.ds(scalars[0] * across + k, 1), :] for k in range(across)], axis=1
    )
    low = jnp.zeros((1, tokens), jnp.float32)
    for number in range(1, DOCS):
        before = jnp.where(docs_in[...] < number, 1.0, 0.0)
        before = jnp.sum(jnp.sum(before, axis=0, keepdims=True), axis=1, keepdims=True)
        low = jnp.where(own_docs == number, before, low)
    low_out[...] = low.astype(jnp.int32)
    route = routes_in[...]
    earlier = lax.broadcasted_iota(jnp.int32, (tokens, tokens), 0)
    earlier = earlier <= lax.broadcasted_iota(jnp.int32, (tokens, tokens), 1)
    named = lax.broadcasted_iota(jnp.int32, (16, tokens), 0) == route
    rank = jnp.dot(
        jnp.where(named, 1.0, 0.0).astype(jnp.bfloat16),
        jnp.where(earlier, 1.0, 0.0).astype(jnp.bfloat16),
        preferred_element_type=jnp.float32,
    )
    rank = rank.astype(jnp.int32) - 1
    number = lax.broadcasted_iota(jnp.int32, (PADDED_CAP, tokens), 0)
    for expert in range(rows // PADDED_CAP):
        placed = (rank[expert : expert + 1, :] == number) & (route == expert)
        table[expert * PADDED_CAP : (expert + 1) * PADDED_CAP, :] = jnp.where(
            placed, 1.0, 0.0
        ).astype(jnp.bfloat16)
    chosen = table[...]
    start = scalars[0] * BLOCK
    place = start + lax.broadcasted_iota(jnp.int32, (1, tokens), 1)
    held = chosen.astype(jnp.float32)
    first = jnp.sum(held * low, axis=1, keepdims=True)
    last = jnp.sum(held * place.astype(jnp.float32), axis=1, keepdims=True)
    slot_low[...] = first.astype(jnp.int32)
    slot_high[...] = jnp.maximum(last.astype(jnp.int32), start)
    for copy in copies[2:]:
        copy.wait()
    picked[...] = jnp.dot(chosen, query[...], preferred_element_type=jnp.float32).astype(
        jnp.bfloat16
    )
    slot_resid[...] = lax.dot_general(
        chosen, features_in[...], (((1,), (1,)), ((), ())), preferred_element_type=jnp.float32
    ).astype(jnp.bfloat16)


def prepare_slots(scalars, queries, routes, docs, residual, rows):
    _, tokens, width = queries.shape
    return pl.pallas_call(
        prepare_kernel,
        out_shape=[
            jax.ShapeDtypeStruct((rows, width), jnp.bfloat16),
            jax.ShapeDtypeStruct((rows, tokens), jnp.bfloat16),
            jax.ShapeDtypeStruct((1, tokens), jnp.int32),
            jax.ShapeDtypeStruct((rows, 1), jnp.int32),
            jax.ShapeDtypeStruct((rows, 1), jnp.int32),
            jax.ShapeDtypeStruct((rows, residual.shape[0]), jnp.bfloat16),
        ],
        in_specs=[SMEM, ANY, ANY, ANY, ANY],
        out_specs=[VMEM] * 6,
        scratch_shapes=[
            pltpu.VMEM((tokens, width), jnp.bfloat16),
            pltpu.VMEM(residual.shape, jnp.bfloat16),
            pltpu.VMEM(routes.shape, jnp.int32),
            pltpu.VMEM(docs.shape, jnp.int32),
            pltpu.SemaphoreType.DMA((4,)),
        ],
        compiler_params=pltpu.CompilerParams(vmem_limit_bytes=40 * MIB),
        cost_estimate=pl.CostEstimate(
            flops=2 * rows * tokens * 4 * width, bytes_accessed=8 * MIB, transcendentals=0
        ),
    )(scalars, queries, routes, docs, residual)


def slots_kernel(scalars, picked, low, slot_low, slot_high, slot_resid, weight, *refs):
    blocks = refs[:KV_SLOTS]
    out, pairs, bias, highest, numer, mix, product, done = refs[KV_SLOTS:]
    copies = fetch(blocks, [pairs.at[n] for n in range(KV_SLOTS)], done)
    span_of = span(scalars, low[...].astype(jnp.float32))
    for copy in copies:
        copy.wait()
    flash(span_of, picked, slot_low[...], slot_high[...], pairs, bias, highest, numer)
    store_heads(numer, mix)
    product[...] = jnp.dot(mix[...], weight[...], preferred_element_type=jnp.float32)
    features = slot_resid.shape[1]
    for part in range(product.shape[1] // features):

        @pl.when(scalars[1] == part)
        def _():
            product[:, part * features : (part + 1) * features] += slot_resid[...].astype(
                jnp.float32
            )

    width = product.shape[1]
    for part in range(out.shape[0]):
        base = part // 2 * PADDED_CAP + part % 2 * SHARE
        whole = SHARE // SUB
        for group in range(whole):
            at = base + group * SUB
            out[part, :, group * width : (group + 1) * width] = product[
                at : at + SUB, :
            ].astype(jnp.bfloat16)
        rest = product[base + whole * SUB : base + SHARE, :]
        rest = jnp.concatenate([rest[:, : width // 2], rest[:, width // 2 :]], axis=0)
        out[part, :, whole * width :] = rest.astype(jnp.bfloat16)


def attend_slots(scalars, picked, low, slot_low, slot_high, slot_resid, weight, blocks):
    rows, width = picked.shape
    out_width = weight.shape[1]
    scratch = flash_scratch(rows, rows, width)
    return pl.pallas_call(
        slots_kernel,
        out_shape=jax.ShapeDtypeStruct(
            (2 * rows // PADDED_CAP, SUB, SHARE * out_width // SUB), jnp.bfloat16
        ),
        in_specs=[SMEM] + [VMEM] * 6 + [ANY] * KV_SLOTS,
        out_specs=VMEM,
        scratch_shapes=[scratch[0], *scratch[2:5]]
        + [
            pltpu.VMEM((rows, width), jnp.bfloat16),
            pltpu.VMEM((rows, out_width), jnp.float32),
            scratch[5],
        ],
        compiler_params=pltpu.CompilerParams(vmem_limit_bytes=SLOTS_VMEM * MIB),
        cost_estimate=flash_cost(rows, 2 * rows * width * out_width, 2 * width * out_width),
    )(scalars, picked, low, slot_low, slot_high, slot_resid, weight, *blocks)


def norm_kernel(shares, gain, *refs):
    out = refs[-1]
    total = shares[0].astype(jnp.float32)
    for number in range(1, shares.shape[0]):
        total = total + shares[number].astype(jnp.float32)
    rows, width = out.shape
    whole = SHARE // SUB
    groups = [total[:, group * width : (group + 1) * width] for group in range(whole)]
    rest = total[:, whole * width :]
    groups.append(jnp.concatenate([rest[: SUB // 2], rest[SUB // 2 :]], axis=1))
    groups.append(jnp.zeros((rows - SHARE, width), jnp.float32))
    state = jnp.concatenate(groups, axis=0)
    mean_square = jnp.mean(state * state, axis=1, keepdims=True)
    out[...] = (state * lax.rsqrt(mean_square + norm_eps) * gain[...]).astype(jnp.bfloat16)


def normalize(shares, norm_gain, after):
    count = shares.shape[0]
    rows, width = HALF, norm_gain.shape[0]
    return pl.pallas_call(
        norm_kernel,
        out_shape=jax.ShapeDtypeStruct((rows, width), jnp.bfloat16),
        in_specs=[VMEM, VMEM] + [VMEM] * len(after),
        out_specs=VMEM,
        compiler_params=pltpu.CompilerParams(vmem_limit_bytes=24 * MIB),
        cost_estimate=pl.CostEstimate(
            flops=count * rows * width * 3,
            bytes_accessed=(count + 1) * rows * width * 2,
            transcendentals=rows,
        ),
    )(shares, norm_gain.reshape(1, width), *after)


def hidden_kernel(offsets, *refs):
    pieces = len(offsets)
    rows_in, weights_in = refs[:pieces], refs[pieces : pieces + 4]
    act, rows, weights, total = refs[pieces + 4 :]
    step = pl.program_id(0)
    units = weights_in[0].shape[0]

    @pl.when(step == 0)
    def _():
        total[...] = jnp.zeros(total.shape, jnp.float32)

    for offset, piece in zip(offsets, rows_in):
        rows[offset : offset + piece.shape[0], :] = piece[...]
    for number in range(4):
        weights[number * units : (number + 1) * units, :] = weights_in[number][...]
    total[...] += lax.dot_general(
        rows[...],
        weights[...],
        (((1,), (1,)), ((), ())),
        preferred_element_type=jnp.float32,
    )

    @pl.when(step == pl.num_programs(0) - 1)
    def _():
        gate = total[:, : 2 * units]
        up = total[:, 2 * units :]
        act[...] = (gate / (1.0 + jnp.exp(-gate)) * up).astype(jnp.bfloat16)


def hidden(row_pieces, weights):
    offsets, flat = [], []
    for number, parts in enumerate(row_pieces):
        offset = number * CAP
        for part in parts:
            offsets.append(offset)
            flat.append(part)
            offset += part.shape[0]
    width = flat[0].shape[1]
    units = weights[0].shape[0]
    rows = len(row_pieces) * CAP
    chunk = 1280
    weight_spec = pl.BlockSpec((units, chunk), lambda i: (0, i))
    return pl.pallas_call(
        functools.partial(hidden_kernel, tuple(offsets)),
        grid=(width // chunk,),
        out_shape=jax.ShapeDtypeStruct((rows, 2 * units), jnp.bfloat16),
        in_specs=[pl.BlockSpec((part.shape[0], chunk), lambda i: (0, i)) for part in flat]
        + [weight_spec] * 4,
        out_specs=pl.BlockSpec((rows, 2 * units), lambda i: (0, 0)),
        scratch_shapes=[
            pltpu.VMEM((rows, chunk), jnp.bfloat16),
            pltpu.VMEM((4 * units, chunk), jnp.bfloat16),
            pltpu.VMEM((rows, 4 * units), jnp.float32),
        ],
        compiler_params=pltpu.CompilerParams(vmem_limit_bytes=40 * MIB),
        cost_estimate=pl.CostEstimate(
            flops=8 * rows * width * units,
            bytes_accessed=2 * rows * width + 8 * width * units,
            transcendentals=2 * rows * units,
        ),
    )(*flat, *weights)


def down_kernel(places, act, down_own, down_other, out, weights, product):
    units = down_own.shape[0]
    pieces, parts = out.shape[:2]
    features = product.shape[1] // parts
    weights[:units, :] = down_own[...]
    weights[units:, :] = down_other[...]
    product[...] = jnp.dot(act[...], weights[...], preferred_element_type=jnp.float32)
    for number in range(pieces):
        place = places[number]
        for part in range(parts):
            for group in range(CAP // SUB):
                at = number * CAP + group * SUB
                out[place, part, :, group * features : (group + 1) * features] = product[
                    at : at + SUB, part * features : (part + 1) * features
                ].astype(jnp.bfloat16)


def down(places, act, downs, parts):
    rows = act.shape[0]
    units, width = downs[0].shape
    pieces = rows // CAP
    packed = (SUB, CAP // SUB * (width // parts))
    steps = 2
    weight_spec = pl.BlockSpec((units, width // steps), lambda i: (0, i))
    return pl.pallas_call(
        down_kernel,
        grid=(steps,),
        out_shape=jax.ShapeDtypeStruct((pieces, parts, *packed), jnp.bfloat16),
        in_specs=[SMEM, pl.BlockSpec(act.shape, lambda i: (0, 0)), weight_spec, weight_spec],
        out_specs=pl.BlockSpec((pieces, parts // steps, *packed), lambda i: (0, i, 0, 0)),
        scratch_shapes=[
            pltpu.VMEM((2 * units, width // steps), jnp.bfloat16),
            pltpu.VMEM((rows, width // steps), jnp.float32),
        ],
        compiler_params=pltpu.CompilerParams(vmem_limit_bytes=48 * MIB),
        cost_estimate=pl.CostEstimate(
            flops=4 * rows * width * units,
            bytes_accessed=2 * rows * width + 4 * width * units,
            transcendentals=0,
        ),
    )(places, act, *downs)


def collect_kernel(shares, table, out, merged):
    step = pl.program_id(0)
    sources, _, halves, sub, packed = shares.shape
    features = merged.shape[2]
    total = jnp.zeros((sub, packed), jnp.float32)
    for source in range(sources):
        for half in range(halves):
            total = total + shares[source, 0, half].astype(jnp.float32)
    groups = [total[:, at : at + features] for at in range(0, packed, features)]
    groups.append(jnp.zeros((PADDED_CAP - CAP, features), jnp.float32))
    merged[step] = jnp.concatenate(groups, axis=0).astype(jnp.bfloat16)

    @pl.when(step == pl.num_programs(0) - 1)
    def _():
        experts = merged.shape[0]
        stacked = merged[...].reshape(experts * PADDED_CAP, features)
        out[...] = lax.dot_general(
            stacked, table[...], (((0,), (0,)), ((), ())), preferred_element_type=jnp.float32
        ).astype(jnp.bfloat16)


def collect(shares, table):
    sources, experts, halves, sub, packed = shares.shape
    features = packed * sub // CAP
    tokens = table.shape[1]
    return pl.pallas_call(
        collect_kernel,
        grid=(experts,),
        out_shape=jax.ShapeDtypeStruct((features, tokens), jnp.bfloat16),
        in_specs=[
            pl.BlockSpec((sources, 1, halves, sub, packed), lambda i: (0, i, 0, 0, 0)),
            pl.BlockSpec(table.shape, lambda i: (0, 0)),
        ],
        out_specs=pl.BlockSpec((features, tokens), lambda i: (0, 0)),
        scratch_shapes=[pltpu.VMEM((experts, PADDED_CAP, features), jnp.bfloat16)],
        compiler_params=pltpu.CompilerParams(vmem_limit_bytes=24 * MIB),
        cost_estimate=pl.CostEstimate(
            flops=2 * tokens * table.shape[0] * features,
            bytes_accessed=2 * shares.size + 2 * tokens * features,
            transcendentals=0,
        ),
    )(shares, table)


def shards(
    queries,
    common_keys,
    common_values,
    doc_ids,
    routes,
    residual,
    out_weight,
    norm_gain,
    gate_weight,
    up_weight,
    down_weight,
):
    ctx_size = lax.axis_size("ctx")
    exp_size = lax.axis_size("exp")
    chips = ctx_size // 2
    in_flight = exp_size // 2
    tokens = queries.shape[1]
    features = residual.shape[1]
    ctx = lax.axis_index("ctx")
    exp = lax.axis_index("exp")
    chip, core = ctx // 2, ctx % 2
    swap_cores = [(c, c ^ 1) for c in range(ctx_size)]

    own = jnp.concatenate([common_keys, common_values], axis=1)
    mine = [own] + [
        lax.ppermute(own, "ctx", [(c, c + 2 * s) for c in range(ctx_size - 2 * s)])
        for s in range(1, BACK + 1)
    ]
    scalars = jnp.stack([ctx, exp]).astype(jnp.int32)
    picked, table, low, slot_low, slot_high, slot_resid = prepare_slots(
        scalars,
        queries,
        routes.reshape(1, tokens),
        doc_ids.reshape(-1, 128),
        residual.T,
        in_flight * PADDED_CAP,
    )
    theirs = [
        lax.ppermute(lax.optimization_barrier((block, slot_high))[0], "ctx", swap_cores)
        for block in mine
    ]
    blocks = mine + theirs
    product = attend_slots(
        scalars, picked, low, slot_low, slot_high, slot_resid, out_weight, blocks
    )
    shares = lax.all_to_all(product, "exp", 0, 0, tiled=True)
    low, _ = lax.optimization_barrier((low, product))
    first_attention, first_done = attend_first(scalars, queries, low.reshape(tokens, 1), blocks)
    gate, up, down_own = gate_weight[0].T, up_weight[0].T, down_weight[0]
    gate, up, down_own, _ = lax.optimization_barrier((gate, up, down_own, low))
    gate_other, up_other, down_other = (
        lax.ppermute(weight, "ctx", swap_cores) for weight in (gate, up, down_own)
    )
    swapped = gate_other[:8, :128] + up_other[:8, :128] + down_other[:8, :128]
    normed = normalize(shares, norm_gain, after=(first_done + swapped.astype(jnp.float32),))

    pair = [(e, e ^ 1) for e in range(exp_size)]
    other = lax.ppermute(normed, "exp", pair)
    odd = exp % 2 == 1
    block = jnp.concatenate(
        [jnp.where(odd, other, normed)[:SHARE], jnp.where(odd, normed, other)[:SHARE]], axis=0
    )
    ring = chips // 2

    def beside(c, distance):
        chip_of, core_of = c // 2, c % 2
        place = (chip_of % ring + distance) % ring
        return (chip_of // ring * ring + place) * 2 + core_of

    right = [(c, beside(c, 1)) for c in range(ctx_size)]
    left = [(c, beside(c, -1)) for c in range(ctx_size)]
    across = [(c, (c + ctx_size // 2) % ctx_size) for c in range(ctx_size)]
    from_left = lax.ppermute(block, "ctx", right)
    from_right = lax.ppermute(block, "ctx", left)
    far = lax.ppermute(block, "ctx", across)
    opposite_top = lax.ppermute(from_left[:SPLIT], "ctx", right)
    opposite_rest = lax.ppermute(from_right[SPLIT:], "ctx", left)
    far_next, _, _ = lax.optimization_barrier((far, from_left, from_right))
    far_left = lax.ppermute(far_next, "ctx", right)
    far_right = lax.ppermute(far_next, "ctx", left)
    far_opposite_top = lax.ppermute(opposite_top, "ctx", across)
    far_opposite_rest = lax.ppermute(opposite_rest, "ctx", across)
    pieces = [
        (block,),
        (far,),
        (from_left,),
        (from_right,),
        (far_left,),
        (far_right,),
        (opposite_top, opposite_rest),
        (far_opposite_top, far_opposite_rest),
    ]
    row, along = chip // ring, chip % ring
    places = jnp.stack(
        [
            (row ^ z) * ring + (along + x) % ring
            for z, x in (
                (0, 0), (1, 0), (0, ring - 1), (0, 1), (1, ring - 1), (1, 1), (0, 2), (1, 2)
            )
        ]
    ).astype(jnp.int32)

    act = hidden(pieces, (gate, gate_other, up, up_other))
    partial = down(places, act, (down_own, down_other), exp_size)
    same_core = [
        [c * exp_size + e for c in range(k, ctx_size, 2) for e in range(exp_size)]
        for k in range(2)
    ]
    returned = lax.all_to_all(
        partial.reshape(chips * exp_size, *partial.shape[2:]),
        ("ctx", "exp"),
        0,
        0,
        tiled=True,
        axis_index_groups=same_core,
    )
    expert_output = collect(returned.reshape(chips, in_flight, 2, *partial.shape[2:]), table)
    return (first_attention, expert_output.T)


def solution(mesh):
    in_specs = (
        P(None, "ctx", "exp"),
        P("ctx", "exp"),
        P("ctx", "exp"),
        P(),
        P("ctx", None),
        P("ctx", "exp"),
        P("exp", None),
        P(),
        P("exp", None, "ctx"),
        P("exp", None, "ctx"),
        P("exp", "ctx", None),
    )
    out_specs = (P("ctx", "exp"), P("ctx", "exp"))
    return jax.shard_map(shards, mesh=mesh, in_specs=in_specs, out_specs=out_specs, check_vma=False)
```
